512 devices in a mesh: pipe: 8 (over z_hi, core), expert: 64 (over z_lo, y, x).
Axes of the slice: x: 4, y: 4, z: 16 (z_hi: 4, z_lo: 4; z = z_hi * 4 + z_lo), core: 2. Of those that a mesh axis runs over, the one named last changes fastest.
Arguments:
- held_acts: bfloat16 [8, 1024, 3584], P('pipe', 'expert'), may hold values from -6 to 6
- held_grads: bfloat16 [8, 1024, 3584], P('pipe', 'expert'), may hold values from -6 to 6
- saved_inputs: bfloat16 [8, 1024, 3584], P('pipe', 'expert'), may hold values from -6 to 6
- norm_gain: float32 [8, 3584], P('pipe'), may hold values from 0.25 to 1.75
- gate_proj: bfloat16 [8, 3584, 8192], P('pipe', None, 'expert'), may hold values from -0.09375 to 0.09375
- up_proj: bfloat16 [8, 3584, 8192], P('pipe', None, 'expert'), may hold values from -0.09375 to 0.09375
- down_proj: bfloat16 [8, 8192, 3584], P('pipe', 'expert'), may hold values from -0.1875 to 0.1875
- fwd_routes: int32 [8, 1024, 2], P('pipe', 'expert'), may hold values from 0 to 7, all different within a row; in each aligned block of 16 rows (0 to 15, 16 to 31, ..., all dimensions but the last counted through in order) at most 6 rows name the same one
- fwd_gates: float32 [8, 1024, 2], P('pipe', 'expert'), may hold values from 0.1 to 1
- bwd_routes: int32 [8, 1024, 2], P('pipe', 'expert'), may hold values from 0 to 7, all different within a row; in each aligned block of 16 rows (0 to 15, 16 to 31, ..., all dimensions but the last counted through in order) at most 6 rows name the same one
- bwd_gates: float32 [8, 1024, 2], P('pipe', 'expert'), may hold values from 0.1 to 1
Outputs:
- section_outputs: bfloat16 [8, 1024, 3584], P('pipe', 'expert')
- input_grads: bfloat16 [8, 1024, 3584], P('pipe', 'expert')
The draws below stay inside these ranges and needn't reach their ends.
Inputs may be any that keep to these rules, and one draw needn't show every extreme that they name: `fwd_routes`: within the rows of one device (aligned blocks of 16 rows) no expert is named by more than 6 tokens, a bound that some block reaches; a token's experts differ. `bwd_routes`: as for fwd_routes.
All inputs are finite; a program needn't handle non-finite values.
Results may differ from the reference program's by a relative error of at most 0.0095.
Values may be sent and summed in bfloat16 or wider, within the bound.
A program may use at most 128 MiB of HBM per device.

```python
import math
import jax
import jax.numpy as jnp
import numpy as np
from jax import lax

D = 3584
FFW = 1024
SLICE = 8
TOPK = 2
TOK_DEV = 16
EXPERTS = 8
MOST = 6
TOKENS = 1024
N_PIPE = 8
N_EXPERT = 64


def block_levels(key, shape, cuts, least, top_value):
    level = 1.0
    for dim, shards_of in cuts:
        heights = jax.random.uniform(jax.random.fold_in(jax.random.fold_in(key, 6), dim), (shards_of,), jnp.float32, least / len(cuts), top_value / len(cuts))
        level = level * jnp.repeat(jnp.exp(heights), shape[dim] // shards_of).reshape((-1,) + (1,) * (len(shape) - 1 - dim))
    return level


def shared_out(own_key, own, number, rows, number_of, top, bound, skew):
    sequence = jax.random.permutation(own_key, number_of)
    crowded, ordinary = load_shares(number_of, rows * top, bound, skew, True), load_shares(number_of, rows * top, bound, skew, False)
    places = jnp.arange(number_of)

    def named(lengths, offset_by):
        used = int((lengths > 0).sum())
        fixed = max(1, used // 4)
        shifted = fixed + (places - fixed + offset_by * (used - fixed)) % max(1, number_of - fixed)
        return jnp.zeros((number_of,), jnp.int32).at[sequence[jnp.where(places < fixed, places, shifted)]].set(jnp.asarray(lengths, jnp.int32))

    lengths = jnp.where(number % 4 == 0, named(crowded, number // 4), named(ordinary, number - number // 4 - 1))
    mixed = jax.random.permutation(jax.random.fold_in(own, 3), number_of)
    source_of, sink = mixed[0:number_of // 2 * 2:2], mixed[1:number_of // 2 * 2:2]
    room = jnp.minimum(lengths[source_of] - 1, bound - lengths[sink]) // 2
    room = jnp.where((source_of == sequence[0]) | (sink == sequence[0]) | (lengths[sink] == 0), 0, jnp.maximum(room, 0))
    shifted = jax.random.randint(jax.random.fold_in(own, 4), (number_of // 2,), 0, 1 << 20) % (room + 1)
    lengths = lengths.at[source_of].add(-shifted).at[sink].add(shifted)
    members = jnp.searchsorted(jnp.cumsum(lengths), jnp.arange(rows * top), side="right").astype(jnp.int32)
    listing = members.reshape(top, rows).T
    listing = listing[jax.random.permutation(jax.random.fold_in(own, 1), rows)]
    offset_by = jax.random.randint(jax.random.fold_in(own, 2), (rows, 1), 0, top)
    return jnp.take_along_axis(listing, (jnp.arange(top)[None, :] + offset_by) % top, axis=1)


def load_shares(amount, total, most, skew, full):
    portions = [(1 << 20) // math.isqrt(rank ** skew) + 1 for rank in range(1, amount + 1)]
    largest = most if full else min(most, max(-(-total // amount), total * portions[0] // sum(portions)))
    least = 1 if total - largest >= amount - 1 else 0
    holding, surplus = [largest] + [least] * (amount - 1), total - largest - least * (amount - 1)
    while surplus > 0:
        movable = [i for i in range(1, amount) if holding[i] < largest] or [i for i in range(1, amount) if holding[i] < most]
        pool, budget = sum([portions[i] for i in movable]), surplus
        for i in movable:
            extra = min(most - holding[i], max(1, budget * portions[i] // pool), surplus)
            holding[i] = holding[i] + extra
            surplus = surplus - extra
    return np.array(holding)


def bell_draw(stream_key, extent, scale, reach, shards=(), kind=jnp.bfloat16):
    level = block_levels(stream_key, extent, shards, -0.22, 0.18) if shards else 1.0
    result = jax.random.normal(stream_key, extent, jnp.float32) * scale * level
    return jnp.minimum(jnp.maximum(result, -reach), reach).astype(kind)


def setup_inputs(seed: int = 0) -> dict:
    key_of = jax.random.split(jax.random.key(seed), 12)
    held_acts = bell_draw(key_of[0], (N_PIPE, TOKENS, D), 1.0, 6.0, ((0, 8), (1, 64)))
    held_grads = bell_draw(key_of[1], (N_PIPE, TOKENS, D), 1.0, 6.0, ((0, 8), (1, 64)))
    saved_inputs = bell_draw(key_of[2], (N_PIPE, TOKENS, D), 1.0, 6.0, ((0, 8), (1, 64)))
    norm_gain = jnp.clip(1.0 + 0.15 * jax.random.normal(key_of[3], (N_PIPE, D), jnp.float32), 0.25, 1.75)
    gate_proj = bell_draw(key_of[4], (N_PIPE, D, EXPERTS * FFW), D ** -0.5, 0.09375, ((0, 8), (2, 64)))
    up_proj = bell_draw(key_of[5], (N_PIPE, D, EXPERTS * FFW), D ** -0.5, 0.09375, ((0, 8), (2, 64)))
    down_proj = bell_draw(key_of[6], (N_PIPE, EXPERTS * FFW, D), FFW ** -0.5, 0.1875, ((0, 8), (1, 64)))
    fwd_routes_keys = jax.random.split(jax.random.fold_in(key_of[7], 1), N_PIPE * TOKENS // TOK_DEV)
    fwd_routes_turns = jax.random.permutation(jax.random.fold_in(key_of[7], 3), N_PIPE * TOKENS // TOK_DEV)
    fwd_routes = jax.vmap(lambda own, number: shared_out(jax.random.fold_in(key_of[7], 2), own, number, TOK_DEV, EXPERTS, TOPK, MOST, 1))(fwd_routes_keys, fwd_routes_turns).reshape((N_PIPE, TOKENS, TOPK))
    fwd_gates = jnp.clip(jnp.exp(math.log(1.0) - 2.3025851 * jax.random.uniform(key_of[8], (N_PIPE, TOKENS, TOPK), jnp.float32) ** block_levels(key_of[8], (N_PIPE, TOKENS, TOPK), ((0, 8), (1, 64)), -0.2, 0.2)), 0.1, 1.0)
    bwd_routes_keys = jax.random.split(jax.random.fold_in(key_of[9], 1), N_PIPE * TOKENS // TOK_DEV)
    bwd_routes_turns = jax.random.permutation(jax.random.fold_in(key_of[9], 3), N_PIPE * TOKENS // TOK_DEV)
    bwd_routes = jax.vmap(lambda own, number: shared_out(jax.random.fold_in(key_of[9], 2), own, number, TOK_DEV, EXPERTS, TOPK, MOST, 1))(bwd_routes_keys, bwd_routes_turns).reshape((N_PIPE, TOKENS, TOPK))
    bwd_gates = jnp.clip(jnp.exp(math.log(1.0) - 2.3025851 * jax.random.uniform(key_of[10], (N_PIPE, TOKENS, TOPK), jnp.float32) ** block_levels(key_of[10], (N_PIPE, TOKENS, TOPK), ((0, 8), (1, 64)), -0.2, 0.2)), 0.1, 1.0)
    return dict(held_acts=held_acts, held_grads=held_grads, saved_inputs=saved_inputs, norm_gain=norm_gain, gate_proj=gate_proj, up_proj=up_proj, down_proj=down_proj, fwd_routes=fwd_routes, fwd_gates=fwd_gates, bwd_routes=bwd_routes, bwd_gates=bwd_gates)


NORM_EPSILON = 1e-06

def slot_tables(routes, gates, experts, most):
    token_count, picks = routes.shape
    chosen = (routes[:, :, None] == jnp.arange(experts, dtype=jnp.int32)[None, None, :]).astype(jnp.float32)
    chosen = chosen.reshape(token_count * picks, experts)
    earlier = jnp.cumsum(chosen, axis=0) - chosen
    places = jnp.arange(most, dtype=jnp.int32).astype(jnp.float32)
    placed = chosen[:, :, None] * (earlier[:, :, None] == places[None, None, :]).astype(jnp.float32)
    placed = placed.reshape(token_count, picks, experts * most)
    expert_selection = lax.optimization_barrier(jnp.sum(placed, axis=1))
    routing_weights = lax.optimization_barrier(jnp.sum(placed * gates[:, :, None].astype(jnp.float32), axis=1))
    return (expert_selection, routing_weights)

def normalize(inputs, gain):
    routing_values = inputs.astype(jnp.float32)
    scale = lax.rsqrt(lax.optimization_barrier(jnp.mean(routing_values * routing_values, axis=-1, keepdims=True)) + NORM_EPSILON)
    return ((routing_values * scale * gain[None, :]).astype(jnp.bfloat16), scale)

def round_half(routing_values):
    halved = routing_values.astype(jnp.bfloat16)
    halved = lax.optimization_barrier(halved)
    return halved.astype(jnp.float32)

def expert_forward(rows, w_gate, w_up, w_down):
    gate = jnp.dot(rows, w_gate, preferred_element_type=jnp.float32)
    upper = jnp.dot(rows, w_up, preferred_element_type=jnp.float32)
    active_hidden = (jax.nn.silu(gate) * upper).astype(jnp.bfloat16)
    count = rows.shape[0]
    width = w_down.shape[1]
    pieces = jnp.einsum('rsh,shd->rsd', active_hidden.reshape(count, SLICE, -1).astype(jnp.float32), w_down.reshape(SLICE, -1, width).astype(jnp.float32))
    return lax.optimization_barrier(jnp.sum(round_half(pieces), axis=1))

def expert_backward(rows, incoming, w_gate, w_up, w_down):
    gate = jnp.dot(rows, w_gate, preferred_element_type=jnp.float32)
    upper = jnp.dot(rows, w_up, preferred_element_type=jnp.float32)
    sigma = jax.nn.sigmoid(gate)
    d_active = jnp.dot(incoming, w_down.T, preferred_element_type=jnp.float32)
    d_gate = (d_active * upper * sigma * (1.0 + gate * (1.0 - sigma))).astype(jnp.bfloat16)
    d_upper = (d_active * gate * sigma).astype(jnp.bfloat16)
    count, width = rows.shape
    pieces = jnp.einsum('rsh,dsh->rsd', d_gate.reshape(count, SLICE, -1).astype(jnp.float32), w_gate.reshape(width, SLICE, -1).astype(jnp.float32))
    pieces = pieces + jnp.einsum('rsh,dsh->rsd', d_upper.reshape(count, SLICE, -1).astype(jnp.float32), w_up.reshape(width, SLICE, -1).astype(jnp.float32))
    return lax.optimization_barrier(jnp.sum(round_half(pieces), axis=1))

def to_slots(expert_selection, routing_values):
    blocks = expert_selection.shape[0]
    expert_slots = jnp.einsum('eoy,eor->eyr', expert_selection, routing_values.astype(jnp.float32)).astype(jnp.bfloat16)
    expert_slots = expert_slots.reshape(blocks, EXPERTS, MOST, D)
    return jnp.transpose(expert_slots, (1, 0, 2, 3)).reshape(EXPERTS, blocks * MOST, D)

def from_slots(routing_weights, results):
    blocks = routing_weights.shape[0]
    rows_per_block = results.reshape(EXPERTS, blocks, MOST, D)
    rows_per_block = jnp.transpose(rows_per_block, (1, 0, 2, 3)).reshape(blocks, EXPERTS * MOST, D)
    return jnp.einsum('pax,pxr->par', routing_weights, rows_per_block, precision=lax.Precision.HIGHEST)

def one_section(items):
    section_in, incoming, saved, gain, gate_proj, up_proj, down_proj, fwd_routes, fwd_gates, bwd_routes, bwd_gates = items
    w_gate = jnp.transpose(gate_proj.reshape(D, EXPERTS, FFW), (1, 0, 2))
    w_up = jnp.transpose(up_proj.reshape(D, EXPERTS, FFW), (1, 0, 2))
    w_down = down_proj.reshape(EXPERTS, FFW, D)
    tables = jax.vmap(slot_tables, in_axes=(0, 0, None, None))
    normed_input, unused_scale = normalize(section_in, gain)
    expert_selection, routing_weights = tables(fwd_routes.reshape(N_EXPERT, TOK_DEV, TOPK), fwd_gates.reshape(N_EXPERT, TOK_DEV, TOPK), EXPERTS, MOST)
    expert_slots = to_slots(expert_selection, normed_input.reshape(N_EXPERT, TOK_DEV, D))
    results = lax.map(lambda group: expert_forward(group[0], group[1], group[2], group[3]), (expert_slots, w_gate, w_up, w_down))
    branch = from_slots(routing_weights, results).reshape(TOKENS, D)
    outputs = (section_in.astype(jnp.float32) + branch).astype(jnp.bfloat16)
    normed_back, scale = normalize(saved, gain)
    select_back, weighs_back = tables(bwd_routes.reshape(N_EXPERT, TOK_DEV, TOPK), bwd_gates.reshape(N_EXPERT, TOK_DEV, TOPK), EXPERTS, MOST)
    slots_rows = to_slots(select_back, normed_back.reshape(N_EXPERT, TOK_DEV, D))
    slots_cot = to_slots(select_back, incoming.reshape(N_EXPERT, TOK_DEV, D))
    grads = lax.map(lambda group: expert_backward(group[0], group[1], group[2], group[3], group[4]), (slots_rows, slots_cot, w_gate, w_up, w_down))
    d_normed = from_slots(weighs_back, grads).reshape(TOKENS, D)
    routing_values = saved.astype(jnp.float32)
    scaled = d_normed * gain[None, :]
    d_input = scale * scaled - routing_values * scale * scale * scale * lax.optimization_barrier(jnp.mean(scaled * routing_values, axis=-1, keepdims=True))
    input_grads = (incoming.astype(jnp.float32) + d_input).astype(jnp.bfloat16)
    return (outputs, input_grads)

def reference(held_acts, held_grads, saved_inputs, norm_gain, gate_proj, up_proj, down_proj, fwd_routes, fwd_gates, bwd_routes, bwd_gates):
    section_in = jnp.roll(held_acts, 1, axis=0)
    incoming = jnp.roll(held_grads, -1, axis=0)
    outputs, input_grads = lax.map(one_section, (section_in, incoming, saved_inputs, norm_gain, gate_proj, up_proj, down_proj, fwd_routes, fwd_gates, bwd_routes, bwd_gates))
    return (outputs, input_grads)
```

```python
import functools

import jax
import jax.numpy as jnp
import numpy as np
from jax import lax
from jax.experimental import pallas as pl
from jax.experimental.pallas import tpu as pltpu
from jax.sharding import PartitionSpec as P

EPS = 1e-06
SIDE = 4
MOST = 6
BF16 = jnp.bfloat16
F32 = jnp.float32


def dot(a, b):
    return lax.dot_general(a, b, (((1,), (0,)), ((), ())), preferred_element_type=F32)


def dot_t(a, b):
    return lax.dot_general(a, b, (((1,), (1,)), ((), ())), preferred_element_type=F32)


def constants(tokens):
    per = SIDE * MOST
    r = np.arange(4 * per)
    half, chunk, src, place = r // (2 * per), r // per % 2, r // MOST % SIDE, r % MOST
    t = np.arange(SIDE * tokens) // tokens
    row_lane = np.broadcast_to((half * MOST + place)[:, None], (4 * per, 128)).astype(np.int32)
    mask = np.stack([(src[:, None] == t[None, :]) & (chunk == c)[:, None] for c in range(2)])
    pick = np.zeros((2, SIDE * per, SIDE * 2 * per))
    for y in range(SIDE):
        for c in range(2):
            for i in range(per):
                pick[c, y * per + i, (y * 2 + c) * per + i] = 1
    lane = np.arange(128)
    lane_expert = np.where(lane % 64 < 48, lane % 64 // MOST, -1).astype(np.int32)
    lane_place = (lane % 64 % MOST).astype(np.float32)
    before = (np.arange(tokens)[:, None] > np.arange(tokens)[None, :]).astype(np.float32)
    return (
        jnp.asarray(row_lane),
        jnp.asarray(mask, BF16),
        jnp.asarray(np.swapaxes(mask, 1, 2), BF16),
        jnp.asarray(pick, BF16),
        jnp.asarray(np.swapaxes(pick, 1, 2), BF16),
        jnp.asarray(np.broadcast_to(lane_expert, (tokens, 128))),
        jnp.asarray(np.broadcast_to(lane_place, (tokens, 128))),
        jnp.asarray(before, BF16),
    )


N_SEMS = 72


def kernel(
    acts, grads, saved_ref, gain_ref, gate_w, up_w, down_w, f_routes, f_gates, b_routes, b_gates,
    row_lane, mask, mask_t, pick, pick_t, lane_expert, lane_place, before,
    out_ref, din_ref,
    in_buf, zbuf, tab, ysend, yrecv, xbuf, w1, wd, part, psend, precv, act, dgu,
    mine, rsopp, rsrecv, rssend, rsin, ypack, yret, zsend, zret, own,
    send_sem, recv_sem, copy_sem,
):
    tokens, width = saved_ref.shape[1], saved_ref.shape[2]
    half_d, chunk = width // 2, width // 4
    rows = xbuf.shape[1] * xbuf.shape[2]
    block = xbuf.shape[2]
    hb = block // 2
    hid = wd.shape[0] // 2
    pipe = lax.axis_index("pipe")
    n_pipe = lax.axis_size("pipe")
    me = lax.axis_index("expert")
    z, y, x = me // (SIDE * SIDE), me // SIDE % SIDE, me % SIDE
    h, yl = y // 2, y % 2
    other = 1 - yl

    def at(zz, yy, xx):
        return (pipe, (zz * SIDE + yy) * SIDE + xx)

    ahead, behind = (lax.rem(pipe + 1, n_pipe), me), (lax.rem(pipe + n_pipe - 1, n_pipe), me)
    zs = [lax.rem(z + k, SIDE) for k in range(SIDE)]
    ys = [lax.rem(y + k, SIDE) for k in range(SIDE)]
    xr, xo, xl = (lax.rem(x + k, SIDE) for k in (1, 2, 3))
    right, left = at(z, y, xr), at(z, y, xl)
    mate = at(z, h * 2 + other, x)
    z_peers = [at(zs[k], y, x) for k in (1, 2, 3)]
    y_peers = [at(z, ys[k], x) for k in (1, 2, 3)]

    barrier = pltpu.get_barrier_semaphore()
    peers = [ahead, behind, right, left] + z_peers + y_peers
    for p in peers:
        pl.semaphore_signal(barrier, inc=1, device_id=p, device_id_type=pl.DeviceIdType.MESH)
    pl.semaphore_wait(barrier, len(peers))

    started = []

    def send(src, dst, to):
        i = len(started)
        c = pltpu.make_async_remote_copy(
            src_ref=src, dst_ref=dst, send_sem=send_sem.at[i], recv_sem=recv_sem.at[i],
            device_id=to, device_id_type=pl.DeviceIdType.MESH,
        )
        c.start()
        started.append(c)
        return c

    local = []

    def fetch(src, dst):
        c = pltpu.make_async_copy(src, dst, copy_sem.at[len(local)])
        c.start()
        local.append(c)
        return c

    F, B, C = 0, 1, 2

    c_acts = send(acts.at[0], in_buf, ahead)
    c_grads = send(grads.at[0], zbuf.at[C, z], behind)

    lane = lax.broadcasted_iota(jnp.int32, (tokens, 128), 1)
    is_f = lane < 64
    le = lane_expert[...]
    fr, fg, br, bg = f_routes[0], f_gates[0], b_routes[0], b_gates[0]
    first = le == jnp.where(is_f, fr[:, 0:1], br[:, 0:1])
    second = le == jnp.where(is_f, fr[:, 1:2], br[:, 1:2])
    weight = jnp.where(first, jnp.where(is_f, fg[:, 0:1], bg[:, 0:1]), 0.0)
    weight = weight + jnp.where(second, jnp.where(is_f, fg[:, 1:2], bg[:, 1:2]), 0.0)
    named = jnp.where(first | second, 1.0, 0.0)
    earlier = dot(before[...], named.astype(BF16))
    tab[z] = jnp.where(earlier == lane_place[...], weight, 0.0)
    c_tab = [send(tab.at[z], tab.at[z], p) for p in z_peers]

    def scale_of(v):
        return lax.rsqrt(jnp.mean(v * v, axis=-1, keepdims=True) + EPS)

    def z_spread(a):
        return [send(zbuf.at[a, z], zbuf.at[a, z], p) for p in z_peers]

    gain = gain_ref[...]
    v = saved_ref[0].astype(F32)
    zbuf[B, z] = (v * scale_of(v) * gain).astype(BF16)
    cz = {B: z_spread(B)}

    def d_half(k):
        return pl.ds(pl.multiple_of(k * half_d, half_d), half_d)

    def hidden(k):
        return pl.ds(pl.multiple_of(k * hid, hid), hid)

    f_gu = [fetch(gate_w.at[0, d_half(yl), :], w1.at[yl, :, 0:hid]),
            fetch(up_w.at[0, d_half(yl), :], w1.at[yl, :, hid:2 * hid])]
    f_d = fetch(down_w.at[0, :, d_half(yl)], wd.at[hidden(yl), :])
    c_gu = [send(gate_w.at[0, d_half(other), :], w1.at[yl, :, 0:hid], mate),
            send(up_w.at[0, d_half(other), :], w1.at[yl, :, hid:2 * hid], mate)]

    c_acts.wait_recv()
    v = in_buf[...].astype(F32)
    zbuf[F, z] = (v * scale_of(v) * gain).astype(BF16)
    cz[F] = z_spread(F)
    c_grads.wait_recv()
    cz[C] = z_spread(C)

    for c in c_tab:
        c.wait_recv()
    table = tab[...].reshape(SIDE * tokens, 128)
    lane96 = lax.broadcasted_iota(jnp.int32, row_lane.shape, 1)
    q = [jnp.where(lane96 == row_lane[...] + (2 * MOST * z + 64 * d), 1.0, 0.0).astype(BF16) for d in (0, 1)]
    chosen = jnp.where(table > 0, 1.0, 0.0).astype(BF16)
    selects = [dot_t(q[d], chosen).astype(BF16) for d in (0, 1)]

    def y_spread(a):
        for c in cz[a]:
            c.wait_recv()
        s = selects[0 if a == F else 1]
        s = [s * mask[c] for c in range(2)]
        for k in range(2):
            got = None
            for c in range(2):
                col = k * half_d + c * chunk
                part_c = dot(s[c], zbuf[a, :, :, col:col + chunk].reshape(SIDE * tokens, chunk))
                got = part_c if got is None else got + part_c
            got = got.astype(BF16)
            ysend[a, k, 0] = got[:2 * SIDE * MOST]
            ysend[a, k, 1] = got[2 * SIDE * MOST:]
        yrecv[a, y] = ysend[a, yl, h]
        return [
            send(ysend.at[a, ys[k] % 2, ys[k] // 2], yrecv.at[a, y], y_peers[k - 1])
            for k in (1, 2, 3)
        ]

    def x_spread(a, cy):
        for c in cy:
            c.wait_recv()
        packed = yrecv[a].reshape(SIDE * yrecv.shape[2], chunk)
        for c in range(2):
            xbuf[a, x, :, c * chunk:(c + 1) * chunk] = dot(pick[c], packed).astype(BF16)
        return [send(xbuf.at[a, x], xbuf.at[a, x], right), send(xbuf.at[a, x], xbuf.at[a, x], left)]

    def x_forward(a, cx):
        cx[0].wait_recv()
        one = send(xbuf.at[a, xl, 0:hb], xbuf.at[a, xl, 0:hb], right)
        cx[1].wait_recv()
        two = send(xbuf.at[a, xr, hb:block], xbuf.at[a, xr, hb:block], left)
        return [one, two]

    def gathered(a, cf):
        for c in cf:
            c.wait_recv()
        return xbuf[a].reshape(rows, half_d)

    cy = {B: y_spread(B)}
    cy[F] = y_spread(F)
    cx = {B: x_spread(B, cy[B])}
    cy[C] = y_spread(C)
    cx[F] = x_spread(F, cy[F])
    c_d = send(down_w.at[0, :, d_half(other)], wd.at[hidden(yl), :], mate)
    cf = {B: x_forward(B, cx[B])}
    cx[C] = x_spread(C, cy[C])
    cf[F] = x_forward(F, cx[F])

    for c in f_gu:
        c.wait()
    for c in c_gu:
        c.wait_recv()

    def gate_up(a):
        r = gathered(a, cf[a])
        psend[a] = dot(r, w1[other]).astype(BF16)
        c = send(psend.at[a], precv.at[a], mate)
        part[a] = dot(r, w1[yl])
        return c

    cp = {B: gate_up(B)}
    cf[C] = x_forward(C, cx[C])
    cp[F] = gate_up(F)

    cp[F].wait_recv()
    gu = part[F] + precv[F].astype(F32)
    gate, up = gu[:, :hid], gu[:, hid:]
    act[yl] = (gate * jax.nn.sigmoid(gate) * up).astype(BF16)
    c_act = send(act.at[yl], act.at[yl], mate)
    f_d.wait()
    c_d.wait_recv()

    r = gathered(C, cf[C])
    psend[C, :, 0:hid] = dot_t(r, wd[hidden(other), :]).astype(BF16)
    cp[C] = send(psend.at[C, :, 0:hid], precv.at[C, :, 0:hid], mate)
    d_part = dot_t(r, wd[hidden(yl), :])

    def reduce_one(d, block_of):
        rsopp[d] = block_of(xo).astype(BF16)
        one = send(rsopp.at[d, 0:hb], rsrecv.at[d, 0], right)
        two = send(rsopp.at[d, hb:block], rsrecv.at[d, 1], left)
        mine[d, 0] = block_of(xr)
        mine[d, 1] = block_of(xl)
        mine[d, 2] = block_of(x)
        return [one, two]

    def reduce_two(d, cr):
        cr[0].wait_recv()
        rssend[d, 0, 0:hb] = (mine[d, 0, 0:hb] + rsrecv[d, 0].astype(F32)).astype(BF16)
        rssend[d, 0, hb:block] = mine[d, 0, hb:block].astype(BF16)
        one = send(rssend.at[d, 0], rsin.at[d, 0], right)
        cr[1].wait_recv()
        rssend[d, 1, hb:block] = (mine[d, 1, hb:block] + rsrecv[d, 1].astype(F32)).astype(BF16)
        rssend[d, 1, 0:hb] = mine[d, 1, 0:hb].astype(BF16)
        two = send(rssend.at[d, 1], rsin.at[d, 1], left)
        return [one, two]

    def y_return(d, cr):
        for c in cr:
            c.wait_recv()
        total = mine[d, 2] + rsin[d, 0].astype(F32) + rsin[d, 1].astype(F32)
        total = total.astype(BF16)
        packed = dot(pick_t[0], total[:, :chunk]) + dot(pick_t[1], total[:, chunk:])
        packed = packed.astype(BF16).reshape(ypack.shape[1:])
        ypack[d] = packed
        yret[d, yl, h] = ypack[d, y]
        return [send(ypack.at[d, ys[k]], yret.at[d, yl, h], y_peers[k - 1]) for k in (1, 2, 3)]

    w_hi = table.astype(BF16)
    w_lo = (table - w_hi.astype(F32)).astype(BF16)

    def z_return(d, cr):
        for c in cr:
            c.wait_recv()
        hi, lo = dot_t(w_hi, q[d]).astype(BF16), dot_t(w_lo, q[d]).astype(BF16)
        for k in range(2):
            slots = yret[d, k].reshape(2 * yret.shape[3], chunk)
            for c in range(2):
                col = k * half_d + c * chunk
                m = mask_t[c]
                got = dot(hi * m, slots) + dot(lo * m, slots)
                own[d, :, :, col:col + chunk] = got.reshape(SIDE, tokens, chunk)
        zsend[d] = own[d].astype(BF16)
        return [send(zsend.at[d, zs[k]], zret.at[d, k - 1], z_peers[k - 1]) for k in (1, 2, 3)]

    def total_of(d, cr):
        s = own[d, z]
        for k, c in enumerate(cr):
            c.wait_recv()
            s = s + zret[d, k].astype(F32)
        return s

    c_act.wait_recv()

    def f_block(k):
        return dot(act[0, pl.ds(pl.multiple_of(k * block, block), block), :], wd[0:hid, :]) + dot(
            act[1, pl.ds(pl.multiple_of(k * block, block), block), :], wd[hid:2 * hid, :])

    cr_f = reduce_one(0, f_block)

    cp[B].wait_recv()
    gu = part[B] + precv[B].astype(F32)
    gate, up = gu[:, :hid], gu[:, hid:]
    sigma = jax.nn.sigmoid(gate)
    by_gate = up * sigma * (1.0 + gate * (1.0 - sigma))
    by_up = gate * sigma
    cp[C].wait_recv()
    d_act = d_part + precv[C, :, 0:hid].astype(F32)
    dgu[yl, :, 0:hid] = (d_act * by_gate).astype(BF16)
    dgu[yl, :, hid:2 * hid] = (d_act * by_up).astype(BF16)
    c_dgu = send(dgu.at[yl], dgu.at[yl], mate)

    cr_f = reduce_two(0, cr_f)

    def b_block(k):
        at_k = pl.ds(pl.multiple_of(k * block, block), block)
        return dot_t(dgu[0, at_k, :], w1[0]) + dot_t(dgu[1, at_k, :], w1[1])

    c_dgu.wait_recv()
    cr_b = reduce_one(1, b_block)
    cr_f = y_return(0, cr_f)
    cr_b = reduce_two(1, cr_b)
    cr_f = z_return(0, cr_f)
    cr_b = y_return(1, cr_b)

    out_ref[0] = (in_buf[...].astype(F32) + total_of(0, cr_f)).astype(BF16)

    cr_b = z_return(1, cr_b)
    v = saved_ref[0].astype(F32)
    scale = scale_of(v)
    dn = total_of(1, cr_b) * gain
    d_in = scale * dn - v * (scale * scale * scale) * jnp.mean(dn * v, axis=-1, keepdims=True)
    din_ref[0] = (zbuf[C, z].astype(F32) + d_in).astype(BF16)

    for c in started:
        c.wait_send()


def local(*args):
    held_acts = args[0]
    tokens, width = held_acts.shape[1:]
    hid = args[4].shape[2]
    per = SIDE * MOST
    block = SIDE * per
    rows = SIDE * block
    half_d, chunk = width // 2, width // 4
    consts = constants(tokens)
    vmem, hbm = pl.BlockSpec(memory_space=pltpu.VMEM), pl.BlockSpec(memory_space=pl.ANY)
    out = jax.ShapeDtypeStruct((1, tokens, width), BF16)
    V = pltpu.VMEM
    return pl.pallas_call(
        kernel,
        out_shape=(out, out),
        in_specs=[hbm, hbm, vmem, vmem, hbm, hbm, hbm] + [vmem] * (4 + len(consts)),
        out_specs=(vmem, vmem),
        scratch_shapes=[
            V((tokens, width), BF16),
            V((3, SIDE, tokens, width), BF16),
            V((SIDE, tokens, 128), F32),
            V((3, 2, 2, 2 * per, chunk), BF16),
            V((3, SIDE, 2 * per, chunk), BF16),
            V((3, SIDE, block, half_d), BF16),
            V((2, half_d, 2 * hid), BF16),
            V((2 * hid, half_d), BF16),
            V((2, rows, 2 * hid), F32),
            V((3, rows, 2 * hid), BF16),
            V((3, rows, 2 * hid), BF16),
            V((2, rows, hid), BF16),
            V((2, rows, 2 * hid), BF16),
            V((2, 3, block, half_d), F32),
            V((2, block, half_d), BF16),
            V((2, 2, block // 2, half_d), BF16),
            V((2, 2, block, half_d), BF16),
            V((2, 2, block, half_d), BF16),
            V((2, SIDE, 2 * per, chunk), BF16),
            V((2, 2, 2, 2 * per, chunk), BF16),
            V((2, SIDE, tokens, width), BF16),
            V((2, SIDE - 1, tokens, width), BF16),
            V((2, SIDE, tokens, width), F32),
            pltpu.SemaphoreType.DMA((N_SEMS,)),
            pltpu.SemaphoreType.DMA((N_SEMS,)),
            pltpu.SemaphoreType.DMA((3,)),
        ],
        compiler_params=pltpu.CompilerParams(
            collective_id=0, has_side_effects=True, vmem_limit_bytes=58 * 1024 * 1024
        ),
    )(*args, *consts)


def solution(mesh):
    return jax.shard_map(
        local,
        mesh=mesh,
        in_specs=(
            P("pipe", "expert", None),
            P("pipe", "expert", None),
            P("pipe", "expert", None),
            P("pipe", None),
            P("pipe", None, "expert"),
            P("pipe", None, "expert"),
            P("pipe", "expert", None),
            P("pipe", "expert", None),
            P("pipe", "expert", None),
            P("pipe", "expert", None),
            P("pipe", "expert", None),
        ),
        out_specs=(P("pipe", "expert", None), P("pipe", "expert", None)),
        check_vma=False,
    )
```

```python
import functools

import jax
import jax.numpy as jnp
import numpy as np
from jax import lax
from jax.experimental import pallas as pl
from jax.experimental.pallas import tpu as pltpu
from jax.sharding import PartitionSpec as P

EPS = 1e-06
SIDE = 4
MOST = 6
BF16 = jnp.bfloat16
F32 = jnp.float32


def dot(a, b):
    return lax.dot_general(a, b, (((1,), (0,)), ((), ())), preferred_element_type=F32)


def dot_t(a, b):
    return lax.dot_general(a, b, (((1,), (1,)), ((), ())), preferred_element_type=F32)


def constants():
    per = SIDE * MOST
    r = np.arange(4 * per)
    half, chunk, plane, place = r // (2 * per), r // per % 2, r // MOST % SIDE, r % MOST
    slot_lane = (2 * plane + half) * MOST + place
    slots = np.zeros((2, 2, 4 * per, 128))
    for d in range(2):
        for c in range(2):
            slots[d, c, r, slot_lane + 64 * d] = chunk == c
    return jnp.asarray(slots, BF16)


def sixth(i):
    return (i * 683) >> 12


def one_hot(shape, place):
    row = lax.broadcasted_iota(jnp.int32, shape, 0)
    col = lax.broadcasted_iota(jnp.int32, shape, 1)
    return jnp.where(place(row, col), 1.0, 0.0).astype(BF16)


N_SEMS = 72


def kernel(
    acts, grads, saved_ref, gain_ref, gate_w, up_w, down_w, f_routes, f_gates, b_routes, b_gates,
    slot_of,
    out_ref, din_ref,
    in_buf, cot_buf, norm_buf, ysend, yrecv, zsend, zrecv, xbuf, w1, wd, part, psend, precv, act,
    dgu, mine, rsopp, rsrecv, rssend, rsin, zpack, zret, ypack, yret,
    pick, pick_t, swap,
    send_sem, recv_sem, copy_sem,
):
    tokens, width = saved_ref.shape[1], saved_ref.shape[2]
    half_d, chunk = width // 2, width // 4
    rows = xbuf.shape[1] * xbuf.shape[2]
    block = xbuf.shape[2]
    hb = block // 2
    hid = wd.shape[0] // 2
    packed_rows = SIDE * yrecv.shape[2]
    pipe = lax.axis_index("pipe")
    n_pipe = lax.axis_size("pipe")
    me = lax.axis_index("expert")
    z, y, x = me // (SIDE * SIDE), me // SIDE % SIDE, me % SIDE
    h, yl = y // 2, y % 2
    other = 1 - yl

    def at(zz, yy, xx):
        return (pipe, (zz * SIDE + yy) * SIDE + xx)

    ahead, behind = (lax.rem(pipe + 1, n_pipe), me), (lax.rem(pipe + n_pipe - 1, n_pipe), me)
    zs = [lax.rem(z + k, SIDE) for k in range(SIDE)]
    ys = [lax.rem(y + k, SIDE) for k in range(SIDE)]
    xr, xo, xl = (lax.rem(x + k, SIDE) for k in (1, 2, 3))
    right, left = at(z, y, xr), at(z, y, xl)
    mate = at(z, h * 2 + other, x)
    z_peers = [at(zs[k], y, x) for k in (1, 2, 3)]
    y_peers = [at(z, ys[k], x) for k in (1, 2, 3)]

    barrier = pltpu.get_barrier_semaphore()
    peers = [ahead, behind, right, left] + z_peers + y_peers
    for p in peers:
        pl.semaphore_signal(barrier, inc=1, device_id=p, device_id_type=pl.DeviceIdType.MESH)
    pl.semaphore_wait(barrier, len(peers))

    started = []

    def send(src, dst, to):
        i = len(started)
        c = pltpu.make_async_remote_copy(
            src_ref=src, dst_ref=dst, send_sem=send_sem.at[i], recv_sem=recv_sem.at[i],
            device_id=to, device_id_type=pl.DeviceIdType.MESH,
        )
        c.start()
        started.append(c)
        return c

    local = []

    def fetch(src, dst):
        c = pltpu.make_async_copy(src, dst, copy_sem.at[len(local)])
        c.start()
        local.append(c)
        return c

    F, B, C = 0, 1, 2

    c_acts = send(acts.at[0], in_buf, ahead)
    c_grads = send(grads.at[0], cot_buf, behind)

    eye = lax.broadcasted_iota(jnp.int32, (tokens, tokens), 0) == lax.broadcasted_iota(
        jnp.int32, (tokens, tokens), 1)
    before = lax.broadcasted_iota(jnp.int32, (tokens, tokens), 0) > lax.broadcasted_iota(
        jnp.int32, (tokens, tokens), 1)
    lane = lax.broadcasted_iota(jnp.int32, (tokens, 128), 1)
    is_f = lane < 64
    lane64 = lane & 63
    lane_expert = (lane64 * 43) >> 8
    lane_place = lane64 - lane_expert * MOST

    def column(ref, k):
        return jnp.sum(jnp.where(eye, ref[0, k:k + 1, :].astype(F32), 0.0), axis=1, keepdims=True)

    le = lane_expert.astype(F32)
    weight, named = 0.0, 0.0
    for k in range(2):
        hit = le == jnp.where(is_f, column(f_routes, k), column(b_routes, k))
        weight = weight + jnp.where(hit, jnp.where(is_f, column(f_gates, k), column(b_gates, k)), 0.0)
        named = named + jnp.where(hit, 1.0, 0.0)
    earlier = dot(jnp.where(before, 1.0, 0.0).astype(BF16), named.astype(BF16))
    table = jnp.where(earlier == lane_place.astype(F32), weight, 0.0)
    chosen = jnp.where(table > 0, 1.0, 0.0).astype(BF16)
    selects = [[dot_t(slot_of[d, c], chosen).astype(BF16) for c in range(2)] for d in range(2)]

    def scale_of(v):
        return lax.rsqrt(jnp.mean(v * v, axis=-1, keepdims=True) + EPS)

    gain = gain_ref[...]

    def y_spread(a, ref):
        s = selects[0 if a == F else 1]
        for k in range(2):
            got = None
            for c in range(2):
                col = k * half_d + c * chunk
                part_c = dot(s[c], ref[:, col:col + chunk])
                got = part_c if got is None else got + part_c
            got = got.astype(BF16)
            ysend[a, k, 0] = got[:yrecv.shape[2]]
            ysend[a, k, 1] = got[yrecv.shape[2]:]
        cs = [
            send(ysend.at[a, ys[k] % 2, ys[k] // 2], yrecv.at[a, y], y_peers[k - 1])
            for k in (1, 2, 3)
        ]
        yrecv[a, y] = ysend[a, yl, h]
        return cs

    def unpacked(i, c):
        return i + (sixth(i) >> 2) * per + c * per

    def swapped(i):
        i6 = sixth(i)
        two = i6 & 3
        return ((two * 2 + ((i6 >> 2) & 1)) * SIDE + (i6 >> 3)) * MOST + i - i6 * MOST

    def z_spread(a, cy):
        for c in cy:
            c.wait_recv()
        got = dot(swap[...], yrecv[a].reshape(packed_rows, chunk)).astype(BF16)
        zsend[a] = got.reshape(zsend.shape[1:])
        cs = [send(zsend.at[a, zs[k]], zrecv.at[a, z], z_peers[k - 1]) for k in (1, 2, 3)]
        zrecv[a, z] = zsend[a, z]
        return cs

    def x_spread(a, cz):
        for c in cz:
            c.wait_recv()
        packed = zrecv[a].reshape(packed_rows, chunk)
        for c in range(2):
            xbuf[a, x, :, c * chunk:(c + 1) * chunk] = dot(pick[c], packed).astype(BF16)
        return [send(xbuf.at[a, x], xbuf.at[a, x], right), send(xbuf.at[a, x], xbuf.at[a, x], left)]

    def x_forward(a, cx):
        cx[0].wait_recv()
        one = send(xbuf.at[a, xl, 0:hb], xbuf.at[a, xl, 0:hb], right)
        cx[1].wait_recv()
        two = send(xbuf.at[a, xr, hb:block], xbuf.at[a, xr, hb:block], left)
        return [one, two]

    def gathered(a, cf):
        for c in cf:
            c.wait_recv()
        return xbuf[a].reshape(rows, half_d)

    v = saved_ref[0].astype(F32)
    norm_buf[B] = (v * scale_of(v) * gain).astype(BF16)
    cy = {B: y_spread(B, norm_buf.at[B])}

    def d_half(k):
        return pl.ds(pl.multiple_of(k * half_d, half_d), half_d)

    def hidden(k):
        return pl.ds(pl.multiple_of(k * hid, hid), hid)

    per = block // SIDE
    swap[...] = one_hot(swap.shape, lambda i, j: j == swapped(i))
    for c in range(2):
        pick[c] = one_hot(pick.shape[1:], lambda i, j: j == unpacked(i, c))
        pick_t[c] = one_hot(pick_t.shape[1:], lambda i, j: i == unpacked(j, c))

    f_gu = [fetch(gate_w.at[0, d_half(yl), :], w1.at[yl, :, 0:hid]),
            fetch(up_w.at[0, d_half(yl), :], w1.at[yl, :, hid:2 * hid])]
    f_d = fetch(down_w.at[0, :, d_half(yl)], wd.at[hidden(yl), :])

    cz = {B: z_spread(B, cy[B])}
    c_acts.wait_recv()
    v = in_buf[...].astype(F32)
    norm_buf[F] = (v * scale_of(v) * gain).astype(BF16)
    cy[F] = y_spread(F, norm_buf.at[F])
    c_grads.wait_recv()
    cy[C] = y_spread(C, cot_buf)
    c_gu = [send(gate_w.at[0, d_half(other), :], w1.at[yl, :, 0:hid], mate),
            send(up_w.at[0, d_half(other), :], w1.at[yl, :, hid:2 * hid], mate)]
    c_d = send(down_w.at[0, :, d_half(other)], wd.at[hidden(yl), :], mate)
    cz[F] = z_spread(F, cy[F])
    cx = {B: x_spread(B, cz[B])}
    cz[C] = z_spread(C, cy[C])
    cf = {B: x_forward(B, cx[B])}
    cx[F] = x_spread(F, cz[F])
    cx[C] = x_spread(C, cz[C])
    cf[F] = x_forward(F, cx[F])

    for c in f_gu:
        c.wait()
    for c in c_gu:
        c.wait_recv()

    def gate_up(a):
        r = gathered(a, cf[a])
        psend[a] = dot(r, w1[other]).astype(BF16)
        c = send(psend.at[a], precv.at[a], mate)
        part[a] = dot(r, w1[yl])
        return c

    cp = {B: gate_up(B)}
    cp[F] = gate_up(F)
    cf[C] = x_forward(C, cx[C])

    cp[F].wait_recv()
    gu = part[F] + precv[F].astype(F32)
    gate, up = gu[:, :hid], gu[:, hid:]
    act[yl] = (gate * jax.nn.sigmoid(gate) * up).astype(BF16)
    c_act = send(act.at[yl], act.at[yl], mate)
    f_d.wait()
    c_d.wait_recv()

    def reduce_one(d, block_of):
        rsopp[d] = block_of(xo).astype(BF16)
        one = send(rsopp.at[d, 0:hb], rsrecv.at[d, 0], right)
        two = send(rsopp.at[d, hb:block], rsrecv.at[d, 1], left)
        mine[d, 0] = block_of(xr)
        mine[d, 1] = block_of(xl)
        mine[d, 2] = block_of(x)
        return [one, two]

    def reduce_two(d, cr):
        cr[0].wait_recv()
        rssend[d, 0, 0:hb] = (mine[d, 0, 0:hb] + rsrecv[d, 0].astype(F32)).astype(BF16)
        rssend[d, 0, hb:block] = mine[d, 0, hb:block].astype(BF16)
        one = send(rssend.at[d, 0], rsin.at[d, 0], right)
        cr[1].wait_recv()
        rssend[d, 1, hb:block] = (mine[d, 1, hb:block] + rsrecv[d, 1].astype(F32)).astype(BF16)
        rssend[d, 1, 0:hb] = mine[d, 1, 0:hb].astype(BF16)
        two = send(rssend.at[d, 1], rsin.at[d, 1], left)
        return [one, two]

    def z_return(d, cr):
        for c in cr:
            c.wait_recv()
        total = mine[d, 2] + rsin[d, 0].astype(F32) + rsin[d, 1].astype(F32)
        total = total.astype(BF16)
        packed = dot(pick_t[0], total[:, :chunk]) + dot(pick_t[1], total[:, chunk:])
        zpack[d] = packed.astype(BF16).reshape(zpack.shape[1:])
        cs = [send(zpack.at[d, zs[k]], zret.at[d, z], z_peers[k - 1]) for k in (1, 2, 3)]
        zret[d, z] = zpack[d, z]
        return cs

    def y_return(d, cr):
        for c in cr:
            c.wait_recv()
        got = dot(swap[...], zret[d].reshape(packed_rows, chunk)).astype(BF16)
        ypack[d] = got.reshape(ypack.shape[1:])
        cs = [send(ypack.at[d, ys[k]], yret.at[d, yl, h], y_peers[k - 1]) for k in (1, 2, 3)]
        yret[d, yl, h] = ypack[d, y]
        return cs

    w_hi = table.astype(BF16)
    w_lo = (table - w_hi.astype(F32)).astype(BF16)

    def combine(d, cr):
        hi = [dot_t(w_hi, slot_of[d, c]).astype(BF16) for c in range(2)]
        lo = [dot_t(w_lo, slot_of[d, c]).astype(BF16) for c in range(2)]
        for c in cr:
            c.wait_recv()
        parts = []
        for k in range(2):
            slots = yret[d, k].reshape(2 * yret.shape[3], chunk)
            for c in range(2):
                parts.append(dot(hi[c], slots) + dot(lo[c], slots))
        return jnp.concatenate(parts, axis=1)

    r = gathered(C, cf[C])
    psend[C, :, 0:hid] = dot_t(r, wd[hidden(other), :]).astype(BF16)
    cp[C] = send(psend.at[C, :, 0:hid], precv.at[C, :, 0:hid], mate)
    d_part = dot_t(r, wd[hidden(yl), :])

    c_act.wait_recv()

    def f_block(k):
        at_k = pl.ds(pl.multiple_of(k * block, block), block)
        return dot(act[0, at_k, :], wd[0:hid, :]) + dot(act[1, at_k, :], wd[hid:2 * hid, :])

    cr_f = reduce_one(0, f_block)

    cp[B].wait_recv()
    gu = part[B] + precv[B].astype(F32)
    gate, up = gu[:, :hid], gu[:, hid:]
    sigma = jax.nn.sigmoid(gate)
    by_gate = up * sigma * (1.0 + gate * (1.0 - sigma))
    by_up = gate * sigma
    cp[C].wait_recv()
    d_act = d_part + precv[C, :, 0:hid].astype(F32)
    dgu[yl, :, 0:hid] = (d_act * by_gate).astype(BF16)
    dgu[yl, :, hid:2 * hid] = (d_act * by_up).astype(BF16)
    c_dgu = send(dgu.at[yl], dgu.at[yl], mate)

    cr_f = reduce_two(0, cr_f)

    def b_block(k):
        at_k = pl.ds(pl.multiple_of(k * block, block), block)
        return dot_t(dgu[0, at_k, :], w1[0]) + dot_t(dgu[1, at_k, :], w1[1])

    c_dgu.wait_recv()
    cr_b = reduce_one(1, b_block)
    cr_f = z_return(0, cr_f)
    cr_b = reduce_two(1, cr_b)
    cr_f = y_return(0, cr_f)
    cr_b = z_return(1, cr_b)

    out_ref[0] = (in_buf[...].astype(F32) + combine(0, cr_f)).astype(BF16)

    cr_b = y_return(1, cr_b)
    v = saved_ref[0].astype(F32)
    scale = scale_of(v)
    dn = combine(1, cr_b) * gain
    d_in = scale * dn - v * (scale * scale * scale) * jnp.mean(dn * v, axis=-1, keepdims=True)
    din_ref[0] = (cot_buf[...].astype(F32) + d_in).astype(BF16)

    for c in started:
        c.wait_send()


def local(*args):
    held_acts = args[0]
    tokens, width = held_acts.shape[1:]
    hid = args[4].shape[2]
    per = SIDE * MOST
    block = SIDE * per
    rows = SIDE * block
    half_d, chunk = width // 2, width // 4
    args = args[:7] + tuple(jnp.swapaxes(a, 1, 2) for a in args[7:])
    vmem, hbm = pl.BlockSpec(memory_space=pltpu.VMEM), pl.BlockSpec(memory_space=pl.ANY)
    out = jax.ShapeDtypeStruct((1, tokens, width), BF16)
    V = pltpu.VMEM
    return pl.pallas_call(
        kernel,
        out_shape=(out, out),
        in_specs=[hbm, hbm, vmem, vmem, hbm, hbm, hbm] + [vmem] * 5,
        out_specs=(vmem, vmem),
        scratch_shapes=[
            V((tokens, width), BF16),
            V((tokens, width), BF16),
            V((2, tokens, width), BF16),
            V((3, 2, 2, 2 * per, chunk), BF16),
            V((3, SIDE, 2 * per, chunk), BF16),
            V((3, SIDE, 2 * per, chunk), BF16),
            V((3, SIDE, 2 * per, chunk), BF16),
            V((3, SIDE, block, half_d), BF16),
            V((2, half_d, 2 * hid), BF16),
            V((2 * hid, half_d), BF16),
            V((2, rows, 2 * hid), F32),
            V((3, rows, 2 * hid), BF16),
            V((3, rows, 2 * hid), BF16),
            V((2, rows, hid), BF16),
            V((2, rows, 2 * hid), BF16),
            V((2, 3, block, half_d), F32),
            V((2, block, half_d), BF16),
            V((2, 2, block // 2, half_d), BF16),
            V((2, 2, block, half_d), BF16),
            V((2, 2, block, half_d), BF16),
            V((2, SIDE, 2 * per, chunk), BF16),
            V((2, SIDE, 2 * per, chunk), BF16),
            V((2, SIDE, 2 * per, chunk), BF16),
            V((2, 2, 2, 2 * per, chunk), BF16),
            V((2, block, 2 * block), BF16),
            V((2, 2 * block, block), BF16),
            V((2 * block, 2 * block), BF16),
            pltpu.SemaphoreType.DMA((N_SEMS,)),
            pltpu.SemaphoreType.DMA((N_SEMS,)),
            pltpu.SemaphoreType.DMA((3,)),
        ],
        compiler_params=pltpu.CompilerParams(
            collective_id=0, has_side_effects=True, vmem_limit_bytes=58 * 1024 * 1024
        ),
    )(*args, constants())


def solution(mesh):
    return jax.shard_map(
        local,
        mesh=mesh,
        in_specs=(
            P("pipe", "expert", None),
            P("pipe", "expert", None),
            P("pipe", "expert", None),
            P("pipe", None),
            P("pipe", None, "expert"),
            P("pipe", None, "expert"),
            P("pipe", "expert", None),
            P("pipe", "expert", None),
            P("pipe", "expert", None),
            P("pipe", "expert", None),
            P("pipe", "expert", None),
        ),
        out_specs=(P("pipe", "expert", None), P("pipe", "expert", None)),
        check_vma=False,
    )
```

```python
import functools

import jax
import jax.numpy as jnp
import numpy as np
from jax import lax
from jax.experimental import pallas as pl
from jax.experimental.pallas import tpu as pltpu
from jax.sharding import PartitionSpec as P

EPS = 1e-06
SIDE = 4
MOST = 6
BF16 = jnp.bfloat16
F32 = jnp.float32


def dot(a, b):
    return lax.dot_general(a, b, (((1,), (0,)), ((), ())), preferred_element_type=F32)


def dot_t(a, b):
    return lax.dot_general(a, b, (((1,), (1,)), ((), ())), preferred_element_type=F32)


def constants():
    per = SIDE * MOST
    r = np.arange(4 * per)
    half, chunk, plane, place = r // (2 * per), r // per % 2, r // MOST % SIDE, r % MOST
    slot_lane = (2 * plane + half) * MOST + place
    slots = np.zeros((2, 2, 4 * per, 128))
    for d in range(2):
        for c in range(2):
            slots[d, c, r, slot_lane + 64 * d] = chunk == c
    return jnp.asarray(slots, BF16)


def sixth(i):
    return (i * 683) >> 12


def one_hot(shape, place):
    row = lax.broadcasted_iota(jnp.int32, shape, 0)
    col = lax.broadcasted_iota(jnp.int32, shape, 1)
    return jnp.where(place(row, col), 1.0, 0.0).astype(BF16)


N_SEMS = 112


def kernel(
    acts, grads, saved_in, gain_in, gate_w, up_w, down_w, fr_in, fg_in, br_in, bg_in, slot_in,
    out_ref, din_ref,
    saved_ref, gain_ref, f_routes, f_gates, b_routes, b_gates, slot_of,
    in_buf, cot_buf, norm_buf, ysend, yrecv, zsend, xbuf, rbuf, w1, wd, part, psend, precv, act,
    dgu, mine, rsopp, rsrecv, rssend, rsin, zpack, zret, ypack, yret,
    pick, pick_t, swap,
    send_sem, recv_sem, copy_sem,
):
    tokens, width = saved_ref.shape[1], saved_ref.shape[2]
    half_d, chunk = width // 2, width // 4
    rows = rbuf.shape[1]
    block = rows // SIDE
    per = block // SIDE
    hid = wd.shape[0] // 2
    packed_rows = 2 * block
    pipe = lax.axis_index("pipe")
    n_pipe = lax.axis_size("pipe")
    me = lax.axis_index("expert")
    z, y, x = me // (SIDE * SIDE), me // SIDE % SIDE, me % SIDE
    h, yl = y // 2, y % 2
    other = 1 - yl

    def at(zz, yy, xx):
        return (pipe, (zz * SIDE + yy) * SIDE + xx)

    ahead, behind = (lax.rem(pipe + 1, n_pipe), me), (lax.rem(pipe + n_pipe - 1, n_pipe), me)
    zs = [lax.rem(z + k, SIDE) for k in range(SIDE)]
    zi = [lax.rem(z + SIDE - k, SIDE) for k in range(SIDE)]
    ys = [lax.rem(y + k, SIDE) for k in range(SIDE)]
    xr, xo, xl = (lax.rem(x + k, SIDE) for k in (1, 2, 3))
    right, left = at(z, y, xr), at(z, y, xl)
    mate = at(z, h * 2 + other, x)
    z_peers = [at(zs[k], y, x) for k in (1, 2, 3)]
    y_peers = [at(z, ys[k], x) for k in (1, 2, 3)]

    barrier = pltpu.get_barrier_semaphore()
    peers = [ahead, behind, right, left] + z_peers + y_peers
    for p in peers:
        pl.semaphore_signal(barrier, inc=1, device_id=p, device_id_type=pl.DeviceIdType.MESH)

    started = []

    def send(src, dst, to):
        i = len(started)
        c = pltpu.make_async_remote_copy(
            src_ref=src, dst_ref=dst, send_sem=send_sem.at[i], recv_sem=recv_sem.at[i],
            device_id=to, device_id_type=pl.DeviceIdType.MESH,
        )
        c.start()
        started.append(c)
        return c

    local = []

    def fetch(src, dst):
        c = pltpu.make_async_copy(src, dst, copy_sem.at[len(local)])
        c.start()
        local.append(c)
        return c

    F, B, C = 0, 1, 2

    inputs = [
        fetch(src, dst)
        for src, dst in (
            (fr_in, f_routes), (fg_in, f_gates), (br_in, b_routes), (bg_in, b_gates),
            (slot_in, slot_of), (saved_in, saved_ref), (gain_in, gain_ref),
        )
    ]
    for c in inputs:
        c.wait()

    eye = lax.broadcasted_iota(jnp.int32, (tokens, tokens), 0) == lax.broadcasted_iota(
        jnp.int32, (tokens, tokens), 1)
    before = lax.broadcasted_iota(jnp.int32, (tokens, tokens), 0) > lax.broadcasted_iota(
        jnp.int32, (tokens, tokens), 1)
    lane = lax.broadcasted_iota(jnp.int32, (tokens, 128), 1)
    is_f = lane < 64
    lane64 = lane & 63
    lane_expert = (lane64 * 43) >> 8
    lane_place = lane64 - lane_expert * MOST

    def column(ref, k):
        return jnp.sum(jnp.where(eye, ref[0, k:k + 1, :].astype(F32), 0.0), axis=1, keepdims=True)

    le = lane_expert.astype(F32)
    weight, named = 0.0, 0.0
    for k in range(2):
        hit = le == jnp.where(is_f, column(f_routes, k), column(b_routes, k))
        weight = weight + jnp.where(hit, jnp.where(is_f, column(f_gates, k), column(b_gates, k)), 0.0)
        named = named + jnp.where(hit, 1.0, 0.0)
    earlier = dot(jnp.where(before, 1.0, 0.0).astype(BF16), named.astype(BF16))
    table = jnp.where(earlier == lane_place.astype(F32), weight, 0.0)
    chosen = jnp.where(table > 0, 1.0, 0.0).astype(BF16)
    selects = [[dot_t(slot_of[d, c], chosen).astype(BF16) for c in range(2)] for d in range(2)]

    def scale_of(v):
        return lax.rsqrt(jnp.mean(v * v, axis=-1, keepdims=True) + EPS)

    gain = gain_ref[...]

    def y_pack(a, ref):
        s = selects[0 if a == F else 1]
        for k in range(2):
            got = None
            for c in range(2):
                col = k * half_d + c * chunk
                part_c = dot(s[c], ref[:, col:col + chunk])
                got = part_c if got is None else got + part_c
            got = got.astype(BF16)
            ysend[a, k, 0] = got[:2 * per]
            ysend[a, k, 1] = got[2 * per:]

    def y_spread(a):
        cs = [
            send(ysend.at[a, ys[k] % 2, ys[k] // 2], yrecv.at[a, y], y_peers[k - 1])
            for k in (1, 2, 3)
        ]
        yrecv[a, y] = ysend[a, yl, h]
        return cs

    def unpacked(i, c):
        return i + (sixth(i) >> 2) * per + c * per

    def swapped(i):
        i6 = sixth(i)
        two = i6 & 3
        return ((two * 2 + ((i6 >> 2) & 1)) * SIDE + (i6 >> 3)) * MOST + i - i6 * MOST

    def z_spread(a, cy):
        for c in cy:
            c.wait_recv()
        got = dot(swap[...], yrecv[a].reshape(packed_rows, chunk)).astype(BF16)
        zsend[a] = got.reshape(zsend.shape[1:])
        cs = [send(zsend.at[a, zs[k]], xbuf.at[a, x, z], z_peers[k - 1]) for k in (1, 2, 3)]
        xbuf[a, x, z] = zsend[a, z]
        return [None] + cs

    xs = [[None] * SIDE for _ in range(3)]
    xf = [[], [], []]

    def x_send(a, i, cz):
        if i > 0:
            cz[i].wait_recv()
        ref = xbuf.at[a, x, zi[i]]
        xs[a][i] = (send(ref, ref, right), send(ref, ref, left))

    def x_forward(a, i):
        xs[a][i][i % 2].wait_recv()
        ref = xbuf.at[a, (xl, xr)[i % 2], zi[i]]
        xf[a].append(send(ref, ref, (right, left)[i % 2]))

    def gathered(a):
        for i in range(SIDE):
            xs[a][i][1 - i % 2].wait_recv()
        for c in xf[a]:
            c.wait_recv()
        for s in range(SIDE):
            packed = xbuf[a, s].reshape(packed_rows, chunk)
            for c in range(2):
                rbuf[a, s * block:(s + 1) * block, c * chunk:(c + 1) * chunk] = dot(
                    pick[c], packed).astype(BF16)
        return rbuf[a]

    v = saved_ref[0].astype(F32)
    norm_buf[B] = (v * scale_of(v) * gain).astype(BF16)
    y_pack(B, norm_buf.at[B])

    pl.semaphore_wait(barrier, len(peers))

    cy = {B: y_spread(B)}

    c_acts = send(acts.at[0], in_buf, ahead)
    c_grads = send(grads.at[0], cot_buf, behind)

    def d_half(k):
        return pl.ds(pl.multiple_of(k * half_d, half_d), half_d)

    def hidden(k):
        return pl.ds(pl.multiple_of(k * hid, hid), hid)

    def weight_rows(ref, lane0, k):
        rows_k = pl.ds(pl.multiple_of(other * half_d + k * chunk, chunk), chunk)
        dst = w1.at[yl, k * chunk:(k + 1) * chunk, lane0:lane0 + hid]
        return send(ref.at[0, rows_k, :], dst, mate)

    c_gu = [weight_rows(gate_w, 0, 0)]
    f_gu = [fetch(gate_w.at[0, d_half(yl), :], w1.at[yl, :, 0:hid]),
            fetch(up_w.at[0, d_half(yl), :], w1.at[yl, :, hid:2 * hid])]
    f_d = fetch(down_w.at[0, :, d_half(yl)], wd.at[hidden(yl), :])

    swap[...] = one_hot(swap.shape, lambda i, j: j == swapped(i))
    for c in range(2):
        pick[c] = one_hot(pick.shape[1:], lambda i, j: j == unpacked(i, c))
        pick_t[c] = one_hot(pick_t.shape[1:], lambda i, j: i == unpacked(j, c))

    cz = {B: z_spread(B, cy[B])}
    x_send(B, 0, cz[B])
    c_acts.wait_recv()
    v = in_buf[...].astype(F32)
    norm_buf[F] = (v * scale_of(v) * gain).astype(BF16)
    y_pack(F, norm_buf.at[F])
    cy[F] = y_spread(F)
    c_grads.wait_recv()
    y_pack(C, cot_buf)
    cy[C] = y_spread(C)
    c_gu += [weight_rows(gate_w, 0, 1), weight_rows(up_w, hid, 0), weight_rows(up_w, hid, 1)]
    c_d = send(down_w.at[0, :, d_half(other)], wd.at[hidden(yl), :], mate)
    for i in (1, 2, 3):
        x_send(B, i, cz[B])
    x_forward(B, 0)
    cz[F] = z_spread(F, cy[F])
    x_send(F, 0, cz[F])
    x_forward(B, 1)
    cz[C] = z_spread(C, cy[C])
    x_forward(B, 2)
    x_forward(B, 3)
    for i in (1, 2, 3):
        x_send(F, i, cz[F])
    x_send(C, 0, cz[C])
    for i in range(SIDE):
        x_forward(F, i)
    for i in (1, 2, 3):
        x_send(C, i, cz[C])

    def gate_up(a):
        r = gathered(a)
        psend[a] = dot(r, w1[other]).astype(BF16)
        c = send(psend.at[a], precv.at[a], mate)
        part[a] = dot(r, w1[yl])
        return c

    for c in f_gu:
        c.wait()
    for c in c_gu:
        c.wait_recv()
    cp = {F: gate_up(F)}
    for i in range(SIDE):
        x_forward(C, i)
    cp[B] = gate_up(B)

    cp[F].wait_recv()
    gu = part[F] + precv[F].astype(F32)
    gate, up = gu[:, :hid], gu[:, hid:]
    act[yl] = (gate * jax.nn.sigmoid(gate) * up).astype(BF16)
    c_act = send(act.at[yl], act.at[yl], mate)

    to_right, to_left = (2, 1), (3, 0)

    def reduce_start(d, block_of):
        rsopp[d] = block_of(xo).astype(BF16).reshape(rsopp.shape[1:])
        opp, got = {}, ({}, {})
        for i, j in zip(to_right, to_left):
            opp[i] = send(rsopp.at[d, zi[i]], rsrecv.at[d, zi[i]], right)
            opp[j] = send(rsopp.at[d, zi[j]], rsrecv.at[d, zi[j]], left)
        for n, (k, to, now) in enumerate(((xr, right, to_left), (xl, left, to_right))):
            mine[d, n] = block_of(k).reshape(mine.shape[2:])
            for i in now:
                rssend[d, n, zi[i]] = mine[d, n, zi[i]].astype(BF16)
                got[n][i] = send(rssend.at[d, n, zi[i]], rsin.at[d, n, zi[i]], to)
        mine[d, 2] = block_of(x).reshape(mine.shape[2:])
        return opp, got

    def reduce_finish(d, cr):
        opp, got = cr
        for pair in zip(to_right, to_left):
            for n, (i, to) in enumerate(zip(pair, (right, left))):
                opp[i].wait_recv()
                total = mine[d, n, zi[i]] + rsrecv[d, zi[i]].astype(F32)
                rssend[d, n, zi[i]] = total.astype(BF16)
                got[n][i] = send(rssend.at[d, n, zi[i]], rsin.at[d, n, zi[i]], to)
        return got

    def z_return(d, got):
        cs = []
        for i in (2, 3, 1, 0):
            got[0][i].wait_recv()
            got[1][i].wait_recv()
            total = mine[d, 2, zi[i]] + rsin[d, 0, zi[i]].astype(F32) + rsin[d, 1, zi[i]].astype(F32)
            if i == 0:
                zret[d, z] = total.astype(BF16)
            else:
                zpack[d, zi[i]] = total.astype(BF16)
                cs.append(send(zpack.at[d, zi[i]], zret.at[d, z], at(zi[i], y, x)))
        return cs

    def y_return(d, cr):
        for c in cr:
            c.wait_recv()
        got = dot(swap[...], zret[d].reshape(packed_rows, chunk)).astype(BF16)
        ypack[d] = got.reshape(ypack.shape[1:])
        cs = [send(ypack.at[d, ys[k]], yret.at[d, yl, h], y_peers[k - 1]) for k in (1, 2, 3)]
        yret[d, yl, h] = ypack[d, y]
        return cs

    w_hi = table.astype(BF16)
    w_lo = (table - w_hi.astype(F32)).astype(BF16)

    def combine(d, cr):
        hi = [dot_t(w_hi, slot_of[d, c]).astype(BF16) for c in range(2)]
        lo = [dot_t(w_lo, slot_of[d, c]).astype(BF16) for c in range(2)]
        for c in cr:
            c.wait_recv()
        parts = []
        for k in range(2):
            slots = yret[d, k].reshape(packed_rows // 2, chunk)
            for c in range(2):
                parts.append(dot(hi[c], slots) + dot(lo[c], slots))
        return jnp.concatenate(parts, axis=1)

    r = gathered(C)
    f_d.wait()
    c_d.wait_recv()
    psend[C, :, 0:hid] = dot_t(r, wd[hidden(other), :]).astype(BF16)
    cp[C] = send(psend.at[C, :, 0:hid], precv.at[C, :, 0:hid], mate)
    d_part = dot_t(r, wd[hidden(yl), :])

    c_act.wait_recv()

    def f_block(k):
        at_k = pl.ds(pl.multiple_of(k * block, block), block)
        a = jnp.concatenate([act[0, at_k, :], act[1, at_k, :]], axis=1)
        total = 0.0
        for c in range(2):
            total = total + dot(dot(pick_t[c], a).astype(BF16), wd[:, c * chunk:(c + 1) * chunk])
        return total

    cr_f = reduce_start(0, f_block)

    cp[B].wait_recv()
    gu = part[B] + precv[B].astype(F32)
    gate, up = gu[:, :hid], gu[:, hid:]
    sigma = jax.nn.sigmoid(gate)
    by_gate = up * sigma * (1.0 + gate * (1.0 - sigma))
    by_up = gate * sigma
    cp[C].wait_recv()
    d_act = d_part + precv[C, :, 0:hid].astype(F32)
    dgu[yl, :, 0:hid] = (d_act * by_gate).astype(BF16)
    dgu[yl, :, hid:2 * hid] = (d_act * by_up).astype(BF16)
    c_dgu = send(dgu.at[yl], dgu.at[yl], mate)

    cr_f = reduce_finish(0, cr_f)

    def b_block(k):
        at_k = pl.ds(pl.multiple_of(k * block, block), block)
        total = 0.0
        for s in range(2):
            for c in range(2):
                a = dot(pick_t[c], dgu[s, at_k, :]).astype(BF16)
                total = total + dot_t(a, w1[s, c * chunk:(c + 1) * chunk, :])
        return total

    c_dgu.wait_recv()
    cr_b = reduce_start(1, b_block)
    cr_f = z_return(0, cr_f)
    cr_b = reduce_finish(1, cr_b)
    cr_f = y_return(0, cr_f)
    cr_b = z_return(1, cr_b)

    out_ref[0] = (in_buf[...].astype(F32) + combine(0, cr_f)).astype(BF16)

    cr_b = y_return(1, cr_b)
    v = saved_ref[0].astype(F32)
    scale = scale_of(v)
    dn = combine(1, cr_b) * gain
    d_in = scale * dn - v * (scale * scale * scale) * jnp.mean(dn * v, axis=-1, keepdims=True)
    din_ref[0] = (cot_buf[...].astype(F32) + d_in).astype(BF16)

    for c in started:
        c.wait_send()


def local(*args):
    held_acts = args[0]
    tokens, width = held_acts.shape[1:]
    hid = args[4].shape[2]
    per = SIDE * MOST
    block = SIDE * per
    rows = SIDE * block
    half_d, chunk = width // 2, width // 4
    args = args[:7] + tuple(jnp.swapaxes(a, 1, 2) for a in args[7:])
    vmem, hbm = pl.BlockSpec(memory_space=pltpu.VMEM), pl.BlockSpec(memory_space=pl.ANY)
    out = jax.ShapeDtypeStruct((1, tokens, width), BF16)
    slots = constants()
    V = pltpu.VMEM
    packed = (SIDE, 2 * per, chunk)
    return pl.pallas_call(
        kernel,
        out_shape=(out, out),
        in_specs=[hbm] * 12,
        out_specs=(vmem, vmem),
        scratch_shapes=[
            V(args[2].shape, BF16),
            V(args[3].shape, F32),
            V(args[7].shape, jnp.int32),
            V(args[8].shape, F32),
            V(args[9].shape, jnp.int32),
            V(args[10].shape, F32),
            V(slots.shape, BF16),
            V((tokens, width), BF16),
            V((tokens, width), BF16),
            V((2, tokens, width), BF16),
            V((3, 2, 2) + packed[1:], BF16),
            V((3,) + packed, BF16),
            V((3,) + packed, BF16),
            V((3, SIDE) + packed, BF16),
            V((3, rows, half_d), BF16),
            V((2, half_d, 2 * hid), BF16),
            V((2 * hid, half_d), BF16),
            V((2, rows, 2 * hid), F32),
            V((3, rows, 2 * hid), BF16),
            V((3, rows, 2 * hid), BF16),
            V((2, rows, hid), BF16),
            V((2, rows, 2 * hid), BF16),
            V((2, 3) + packed, F32),
            V((2,) + packed, BF16),
            V((2,) + packed, BF16),
            V((2, 2) + packed, BF16),
            V((2, 2) + packed, BF16),
            V((2,) + packed, BF16),
            V((2,) + packed, BF16),
            V((2,) + packed, BF16),
            V((2, 2, 2) + packed[1:], BF16),
            V((2, block, 2 * block), BF16),
            V((2, 2 * block, block), BF16),
            V((2 * block, 2 * block), BF16),
            pltpu.SemaphoreType.DMA((N_SEMS,)),
            pltpu.SemaphoreType.DMA((N_SEMS,)),
            pltpu.SemaphoreType.DMA((10,)),
        ],
        compiler_params=pltpu.CompilerParams(
            collective_id=0, has_side_effects=True, vmem_limit_bytes=58 * 1024 * 1024
        ),
    )(*args, slots)


def solution(mesh):
    return jax.shard_map(
        local,
        mesh=mesh,
        in_specs=(
            P("pipe", "expert", None),
            P("pipe", "expert", None),
            P("pipe", "expert", None),
            P("pipe", None),
            P("pipe", None, "expert"),
            P("pipe", None, "expert"),
            P("pipe", "expert", None),
            P("pipe", "expert", None),
            P("pipe", "expert", None),
            P("pipe", "expert", None),
            P("pipe", "expert", None),
        ),
        out_specs=(P("pipe", "expert", None), P("pipe", "expert", None)),
        check_vma=False,
    )
```

```python
import functools

import jax
import jax.numpy as jnp
import numpy as np
from jax import lax
from jax.experimental import pallas as pl
from jax.experimental.pallas import tpu as pltpu
from jax.sharding import PartitionSpec as P

EPS = 1e-06
SIDE = 4
MOST = 6
BF16 = jnp.bfloat16
F32 = jnp.float32


def dot(a, b):
    return lax.dot_general(a, b, (((1,), (0,)), ((), ())), preferred_element_type=F32)


def dot_t(a, b):
    return lax.dot_general(a, b, (((1,), (1,)), ((), ())), preferred_element_type=F32)


def constants():
    per = SIDE * MOST
    r = np.arange(2 * SIDE * per)
    plane, place = r // (2 * per), r % MOST
    slots = np.zeros((2, 2, len(r), 128))
    for h in range(2):
        for d in range(2):
            slots[h, d, r, (2 * plane + h) * MOST + place + 64 * d] = 1
    return jnp.asarray(slots, BF16)


def sixth(i):
    return (i * 683) >> 12


def one_hot(shape, place):
    row = lax.broadcasted_iota(jnp.int32, shape, 0)
    col = lax.broadcasted_iota(jnp.int32, shape, 1)
    return jnp.where(place(row, col), 1.0, 0.0).astype(BF16)


N_SEMS = 128


def kernel(
    acts, grads, saved_in, gain_in, gate_w, up_w, down_w, fr_in, fg_in, br_in, bg_in, slot_in,
    out_ref, din_ref,
    saved_ref, gain_ref, f_routes, f_gates, b_routes, b_gates, slot_of,
    in_buf, cot_buf, norm_buf, tab, ytok, zsend, xbuf, rbuf, w1, wd, part, d_part, psend, precv,
    psend_c, precv_c, act, dgu, mine, rsopp, rsrecv, rssend, rsin, zpack, zret, ypack, yret,
    pick, pick_t,
    send_sem, recv_sem, copy_sem,
):
    tokens, width = saved_ref.shape[1], saved_ref.shape[2]
    half_d, chunk = width // 2, width // 4
    rows = rbuf.shape[1]
    block = rows // SIDE
    per = block // SIDE
    hid = wd.shape[0] // 2
    packed_rows = 2 * block
    pipe = lax.axis_index("pipe")
    n_pipe = lax.axis_size("pipe")
    me = lax.axis_index("expert")
    z, y, x = me // (SIDE * SIDE), me // SIDE % SIDE, me % SIDE
    h, yl = y // 2, y % 2
    other = 1 - yl

    def at(zz, yy, xx):
        return (pipe, (zz * SIDE + yy) * SIDE + xx)

    ahead, behind = (lax.rem(pipe + 1, n_pipe), me), (lax.rem(pipe + n_pipe - 1, n_pipe), me)
    zi = [z, z + 1 - 2 * (z % 2), lax.rem(z + 2, SIDE), SIDE - 1 - z]
    ys = [y, y + 1 - 2 * (y % 2), SIDE - 1 - y, lax.rem(y + 2, SIDE)]
    xr, xo, xl = (lax.rem(x + k, SIDE) for k in (1, 2, 3))
    right, left = at(z, y, xr), at(z, y, xl)
    mate = at(z, h * 2 + other, x)
    z_peers = [at(zi[k], y, x) for k in (1, 2, 3)]
    y_peers = [at(z, ys[k], x) for k in (1, 2, 3)]

    barrier = pltpu.get_barrier_semaphore()
    peers = [ahead, behind, right, left] + z_peers + y_peers
    for p in peers:
        pl.semaphore_signal(barrier, inc=1, device_id=p, device_id_type=pl.DeviceIdType.MESH)

    started = []

    def send(src, dst, to):
        i = len(started)
        c = pltpu.make_async_remote_copy(
            src_ref=src, dst_ref=dst, send_sem=send_sem.at[i], recv_sem=recv_sem.at[i],
            device_id=to, device_id_type=pl.DeviceIdType.MESH,
        )
        c.start()
        started.append(c)
        return c

    local = []

    def fetch(src, dst):
        c = pltpu.make_async_copy(src, dst, copy_sem.at[len(local)])
        c.start()
        local.append(c)
        return c

    F, B, C = 0, 1, 2

    inputs = [
        fetch(src, dst)
        for src, dst in (
            (fr_in, f_routes), (fg_in, f_gates), (br_in, b_routes), (bg_in, b_gates),
            (slot_in.at[h], slot_of), (saved_in, saved_ref), (gain_in, gain_ref),
        )
    ]
    for c in inputs:
        c.wait()

    eye = lax.broadcasted_iota(jnp.int32, (tokens, tokens), 0) == lax.broadcasted_iota(
        jnp.int32, (tokens, tokens), 1)
    before = lax.broadcasted_iota(jnp.int32, (tokens, tokens), 0) > lax.broadcasted_iota(
        jnp.int32, (tokens, tokens), 1)
    lane = lax.broadcasted_iota(jnp.int32, (tokens, 128), 1)
    is_f = lane < 64
    lane64 = lane & 63
    lane_expert = (lane64 * 43) >> 8
    lane_place = lane64 - lane_expert * MOST

    def column(ref, k):
        return jnp.sum(jnp.where(eye, ref[0, k:k + 1, :].astype(F32), 0.0), axis=1, keepdims=True)

    le = lane_expert.astype(F32)
    weight, named = 0.0, 0.0
    for k in range(2):
        hit = le == jnp.where(is_f, column(f_routes, k), column(b_routes, k))
        weight = weight + jnp.where(hit, jnp.where(is_f, column(f_gates, k), column(b_gates, k)), 0.0)
        named = named + jnp.where(hit, 1.0, 0.0)
    earlier = dot(jnp.where(before, 1.0, 0.0).astype(BF16), named.astype(BF16))
    tab[y] = jnp.where(earlier == lane_place.astype(F32), weight, 0.0)

    def scale_of(v):
        return lax.rsqrt(jnp.mean(v * v, axis=-1, keepdims=True) + EPS)

    gain = gain_ref[...]

    def d_half(k):
        return pl.ds(pl.multiple_of(k * half_d, half_d), half_d)

    def y_spread(a, ref):
        cs = [
            send(ref.at[:, d_half(ys[k] % 2)], ytok.at[a, y], y_peers[k - 1]) for k in (1, 2, 3)
        ]
        ytok[a, y] = ref[:, d_half(yl)]
        return cs

    def unpacked(i, c):
        return i + (sixth(i) >> 2) * per + c * per

    def z_spread(a, cy):
        for c in cy:
            c.wait_recv()
        got = 0.0
        for c in range(2):
            toks = ytok[a, :, :, c * chunk:(c + 1) * chunk].reshape(SIDE * tokens, chunk)
            got = got + dot(selects[0 if a == F else 1][c], toks)
        zsend[a] = got.astype(BF16).reshape(zsend.shape[1:])
        cs = [send(zsend.at[a, zi[k]], xbuf.at[a, x, z], z_peers[k - 1]) for k in (1, 2, 3)]
        xbuf[a, x, z] = zsend[a, z]
        return [None] + cs

    xs = [[None] * SIDE for _ in range(3)]
    xf = [[], [], []]

    def x_send(a, i, cz):
        if i > 0:
            cz[i].wait_recv()
        ref = xbuf.at[a, x, zi[i]]
        xs[a][i] = (send(ref, ref, right), send(ref, ref, left))

    def x_forward(a, i):
        xs[a][i][i % 2].wait_recv()
        ref = xbuf.at[a, (xl, xr)[i % 2], zi[i]]
        xf[a].append(send(ref, ref, (right, left)[i % 2]))

    def gathered(a):
        for i in range(SIDE):
            xs[a][i][1 - i % 2].wait_recv()
        for c in xf[a]:
            c.wait_recv()
        for s in range(SIDE):
            packed = xbuf[a, s].reshape(packed_rows, chunk)
            for c in range(2):
                rbuf[a, s * block:(s + 1) * block, c * chunk:(c + 1) * chunk] = dot(
                    pick[c], packed).astype(BF16)

    v = saved_ref[0].astype(F32)
    norm_buf[B] = (v * scale_of(v) * gain).astype(BF16)
    pl.semaphore_wait(barrier, len(peers))

    c_acts = send(acts.at[0], in_buf, ahead)
    c_grads = send(grads.at[0], cot_buf, behind)
    c_tab = [send(tab.at[y], tab.at[y], p) for p in y_peers]
    cy = {B: y_spread(B, norm_buf.at[B])}

    def hidden(k):
        return pl.ds(pl.multiple_of(k * hid, hid), hid)

    def weight_rows(ref, lane0, k):
        rows_k = pl.ds(pl.multiple_of(other * half_d + k * chunk, chunk), chunk)
        dst = w1.at[yl, k * chunk:(k + 1) * chunk, lane0:lane0 + hid]
        return send(ref.at[0, rows_k, :], dst, mate)

    c_gu = [weight_rows(gate_w, 0, 0)]
    def down_piece(q):
        n = hid // SIDE
        rows_q = pl.ds(pl.multiple_of(yl * hid + q * n, n), n)
        return send(down_w.at[0, q * n:(q + 1) * n, d_half(other)], wd.at[rows_q, :], mate)

    f_gu = [fetch(gate_w.at[0, d_half(yl), :], w1.at[yl, :, 0:hid]),
            fetch(up_w.at[0, d_half(yl), :], w1.at[yl, :, hid:2 * hid])]
    f_d = fetch(down_w.at[0, :, d_half(yl)], wd.at[hidden(yl), :])

    for c in range(2):
        pick[c] = one_hot(pick.shape[1:], lambda i, j: j == unpacked(i, c))
        pick_t[c] = one_hot(pick_t.shape[1:], lambda i, j: i == unpacked(j, c))

    for c in c_tab:
        c.wait_recv()
    table = tab[...].reshape(SIDE * tokens, 128)
    chosen = jnp.where(table > 0, 1.0, 0.0).astype(BF16)
    w_hi = table.astype(BF16)
    w_lo = (table - w_hi.astype(F32)).astype(BF16)

    def matches(shape, dim, c):
        row = lax.broadcasted_iota(jnp.int32, shape, dim)
        token = lax.broadcasted_iota(jnp.int32, shape, 1 - dim)
        return ((sixth(row) >> 2) & 1 == c) & (sixth(row) & 3 == token // tokens)

    to_rows, to_tokens = (packed_rows, SIDE * tokens), (SIDE * tokens, packed_rows)
    selects = [
        [jnp.where(matches(to_rows, 0, c), dot_t(slot_of[d], chosen), 0.0).astype(BF16) for c in range(2)]
        for d in range(2)
    ]

    cz = {B: z_spread(B, cy[B])}
    x_send(B, 0, cz[B])
    c_acts.wait_recv()
    v = in_buf[...].astype(F32)
    norm_buf[F] = (v * scale_of(v) * gain).astype(BF16)
    cy[F] = y_spread(F, norm_buf.at[F])
    c_grads.wait_recv()
    cy[C] = y_spread(C, cot_buf)
    c_gu += [weight_rows(gate_w, 0, 1), weight_rows(up_w, hid, 0), weight_rows(up_w, hid, 1)]
    c_d = [down_piece(q) for q in (0, 1)]
    x_send(B, 1, cz[B])
    x_forward(B, 0)
    x_send(B, 2, cz[B])
    cz[F] = z_spread(F, cy[F])
    x_send(F, 0, cz[F])
    x_forward(B, 1)
    x_send(B, 3, cz[B])
    cz[C] = z_spread(C, cy[C])
    x_send(C, 0, cz[C])
    x_forward(B, 2)
    x_send(F, 1, cz[F])
    x_forward(B, 3)
    x_forward(F, 0)
    x_send(F, 2, cz[F])
    x_forward(F, 1)
    x_send(F, 3, cz[F])
    x_forward(C, 0)
    x_forward(F, 2)
    x_send(C, 1, cz[C])
    x_forward(F, 3)
    x_send(C, 2, cz[C])
    x_forward(C, 1)
    x_send(C, 3, cz[C])
    gathered(B)

    order = (xo, xr, xl, x)

    def pair(src, dst):
        return [send(src.at[k], dst.at[k], mate) for k in order]

    def in_blocks(v):
        return v.reshape(SIDE, block, v.shape[1])

    gathered(F)
    for c in f_gu:
        c.wait()
    for c in c_gu:
        c.wait_recv()
    cp = {}
    psend[F] = in_blocks(dot(rbuf[F], w1[other])).astype(BF16)
    cp[F] = pair(psend.at[F], precv.at[F])
    c_d += [down_piece(q) for q in (2, 3)]
    part[F] = in_blocks(dot(rbuf[F], w1[yl]))
    x_forward(C, 2)

    c_act = []
    for n, k in enumerate(order):
        cp[F][n].wait_recv()
        gu = part[F, k] + precv[F, k].astype(F32)
        gate, up = gu[:, :hid], gu[:, hid:]
        act[yl, k] = (gate * jax.nn.sigmoid(gate) * up).astype(BF16)
        c_act.append(send(act.at[yl, k], act.at[yl, k], mate))
        if n == 0:
            x_forward(C, 3)

    psend[B] = in_blocks(dot(rbuf[B], w1[other])).astype(BF16)
    part[B] = in_blocks(dot(rbuf[B], w1[yl]))

    to_right, to_left = (2, 1), (3, 0)

    def reduce_start(d, block_of, ready):
        ready[0].wait_recv()
        rsopp[d] = block_of(xo).astype(BF16).reshape(rsopp.shape[1:])
        opp, got = {}, ({}, {})
        for i, j in zip(to_right, to_left):
            opp[i] = send(rsopp.at[d, zi[i]], rsrecv.at[d, zi[i]], right)
            opp[j] = send(rsopp.at[d, zi[j]], rsrecv.at[d, zi[j]], left)
        for n, (k, to, now) in enumerate(((xr, right, to_left), (xl, left, to_right))):
            ready[n + 1].wait_recv()
            mine[d, n] = block_of(k).reshape(mine.shape[2:])
            for i in now:
                rssend[d, n, zi[i]] = mine[d, n, zi[i]].astype(BF16)
                got[n][i] = send(rssend.at[d, n, zi[i]], rsin.at[d, n, zi[i]], to)
        ready[3].wait_recv()
        mine[d, 2] = block_of(x).reshape(mine.shape[2:])
        return opp, got

    def reduce_finish(d, cr):
        opp, got = cr
        for pair in zip(to_right, to_left):
            for n, (i, to) in enumerate(zip(pair, (right, left))):
                opp[i].wait_recv()
                total = mine[d, n, zi[i]] + rsrecv[d, zi[i]].astype(F32)
                rssend[d, n, zi[i]] = total.astype(BF16)
                got[n][i] = send(rssend.at[d, n, zi[i]], rsin.at[d, n, zi[i]], to)
        return got

    def z_return(d, got):
        cs = []
        for i in (2, 3, 1, 0):
            got[0][i].wait_recv()
            got[1][i].wait_recv()
            total = mine[d, 2, zi[i]] + rsin[d, 0, zi[i]].astype(F32) + rsin[d, 1, zi[i]].astype(F32)
            if i == 0:
                zret[d, z] = total.astype(BF16)
            else:
                zpack[d, zi[i]] = total.astype(BF16)
                cs.append(send(zpack.at[d, zi[i]], zret.at[d, z], at(zi[i], y, x)))
        return cs

    def y_return(d, cr):
        weighs = [
            [jnp.where(matches(to_tokens, 1, c), dot_t(w, slot_of[d]), 0.0).astype(BF16) for w in (w_hi, w_lo)]
            for c in range(2)
        ]
        for c in cr:
            c.wait_recv()
        slots = zret[d].reshape(packed_rows, chunk)
        for c in range(2):
            got = dot(weighs[c][0], slots) + dot(weighs[c][1], slots)
            ypack[d, :, :, c * chunk:(c + 1) * chunk] = got.astype(BF16).reshape(SIDE, tokens, chunk)
        cs = [send(ypack.at[d, ys[k]], yret.at[d, h, :, d_half(yl)], y_peers[k - 1]) for k in (1, 2, 3)]
        yret[d, h, :, d_half(yl)] = ypack[d, y]
        return cs

    def combine(d, cr):
        for c in cr:
            c.wait_recv()
        return yret[d, 0].astype(F32) + yret[d, 1].astype(F32)

    gathered(C)
    f_d.wait()
    for c in c_d:
        c.wait_recv()
    psend_c[...] = in_blocks(dot_t(rbuf[C], wd[hidden(other), :])).astype(BF16)
    cp[C] = pair(psend_c, precv_c)
    cp[B] = pair(psend.at[B], precv.at[B])
    d_part[...] = in_blocks(dot_t(rbuf[C], wd[hidden(yl), :]))

    def f_block(k):
        a = jnp.concatenate([act[0, k], act[1, k]], axis=1)
        total = 0.0
        for c in range(2):
            total = total + dot(dot(pick_t[c], a).astype(BF16), wd[:, c * chunk:(c + 1) * chunk])
        return total

    cr_f = reduce_start(0, f_block, c_act)
    cr_f = reduce_finish(0, cr_f)

    c_dgu = []
    for n, k in enumerate(order):
        cp[C][n].wait_recv()
        cp[B][n].wait_recv()
        gu = part[B, k] + precv[B, k].astype(F32)
        gate, up = gu[:, :hid], gu[:, hid:]
        sigma = jax.nn.sigmoid(gate)
        d_act = d_part[k] + precv_c[k].astype(F32)
        dgu[yl, k, :, 0:hid] = (d_act * up * sigma * (1.0 + gate * (1.0 - sigma))).astype(BF16)
        dgu[yl, k, :, hid:2 * hid] = (d_act * gate * sigma).astype(BF16)
        c_dgu.append(send(dgu.at[yl, k], dgu.at[yl, k], mate))

    def b_block(k):
        total = 0.0
        for s in range(2):
            for c in range(2):
                a = dot(pick_t[c], dgu[s, k]).astype(BF16)
                total = total + dot_t(a, w1[s, c * chunk:(c + 1) * chunk, :])
        return total

    cr_b = reduce_start(1, b_block, c_dgu)
    cr_f = z_return(0, cr_f)
    cr_b = reduce_finish(1, cr_b)
    cr_f = y_return(0, cr_f)
    cr_b = z_return(1, cr_b)

    out_ref[0] = (in_buf[...].astype(F32) + combine(0, cr_f)).astype(BF16)

    cr_b = y_return(1, cr_b)
    v = saved_ref[0].astype(F32)
    scale = scale_of(v)
    dn = combine(1, cr_b) * gain
    d_in = scale * dn - v * (scale * scale * scale) * jnp.mean(dn * v, axis=-1, keepdims=True)
    din_ref[0] = (cot_buf[...].astype(F32) + d_in).astype(BF16)

    for c in started:
        c.wait_send()


def local(*args):
    held_acts = args[0]
    tokens, width = held_acts.shape[1:]
    hid = args[4].shape[2]
    per = SIDE * MOST
    block = SIDE * per
    rows = SIDE * block
    half_d, chunk = width // 2, width // 4
    args = args[:7] + tuple(jnp.swapaxes(a, 1, 2) for a in args[7:])
    vmem, hbm = pl.BlockSpec(memory_space=pltpu.VMEM), pl.BlockSpec(memory_space=pl.ANY)
    out = jax.ShapeDtypeStruct((1, tokens, width), BF16)
    slots = constants()
    V = pltpu.VMEM
    packed = (SIDE, 2 * per, chunk)
    return pl.pallas_call(
        kernel,
        out_shape=(out, out),
        in_specs=[hbm] * 12,
        out_specs=(vmem, vmem),
        scratch_shapes=[
            V(args[2].shape, BF16),
            V(args[3].shape, F32),
            V(args[7].shape, jnp.int32),
            V(args[8].shape, F32),
            V(args[9].shape, jnp.int32),
            V(args[10].shape, F32),
            V(slots.shape[1:], BF16),
            V((tokens, width), BF16),
            V((tokens, width), BF16),
            V((2, tokens, width), BF16),
            V((SIDE, tokens, 128), F32),
            V((3, SIDE, tokens, half_d), BF16),
            V((3,) + packed, BF16),
            V((3, SIDE) + packed, BF16),
            V((3, rows, half_d), BF16),
            V((2, half_d, 2 * hid), BF16),
            V((2 * hid, half_d), BF16),
            V((2, SIDE, block, 2 * hid), F32),
            V((SIDE, block, hid), F32),
            V((2, SIDE, block, 2 * hid), BF16),
            V((2, SIDE, block, 2 * hid), BF16),
            V((SIDE, block, hid), BF16),
            V((SIDE, block, hid), BF16),
            V((2, SIDE, block, hid), BF16),
            V((2, SIDE, block, 2 * hid), BF16),
            V((2, 3) + packed, F32),
            V((2,) + packed, BF16),
            V((2,) + packed, BF16),
            V((2, 2) + packed, BF16),
            V((2, 2) + packed, BF16),
            V((2,) + packed, BF16),
            V((2,) + packed, BF16),
            V((2, SIDE, tokens, half_d), BF16),
            V((2, 2, tokens, width), BF16),
            V((2, block, 2 * block), BF16),
            V((2, 2 * block, block), BF16),
            pltpu.SemaphoreType.DMA((N_SEMS,)),
            pltpu.SemaphoreType.DMA((N_SEMS,)),
            pltpu.SemaphoreType.DMA((10,)),
        ],
        compiler_params=pltpu.CompilerParams(
            collective_id=0, has_side_effects=True, vmem_limit_bytes=58 * 1024 * 1024
        ),
    )(*args, slots)


def solution(mesh):
    return jax.shard_map(
        local,
        mesh=mesh,
        in_specs=(
            P("pipe", "expert", None),
            P("pipe", "expert", None),
            P("pipe", "expert", None),
            P("pipe", None),
            P("pipe", None, "expert"),
            P("pipe", None, "expert"),
            P("pipe", "expert", None),
            P("pipe", "expert", None),
            P("pipe", "expert", None),
            P("pipe", "expert", None),
            P("pipe", "expert", None),
        ),
        out_specs=(P("pipe", "expert", None), P("pipe", "expert", None)),
        check_vma=False,
    )
```

```python
import functools

import jax
import jax.numpy as jnp
import numpy as np
from jax import lax
from jax.experimental import pallas as pl
from jax.experimental.pallas import tpu as pltpu
from jax.sharding import PartitionSpec as P

EPS = 1e-06
SIDE = 4
MOST = 6
BF16 = jnp.bfloat16
F32 = jnp.float32


def dot(a, b):
    return lax.dot_general(a, b, (((1,), (0,)), ((), ())), preferred_element_type=F32)


def dot_t(a, b):
    return lax.dot_general(a, b, (((1,), (1,)), ((), ())), preferred_element_type=F32)


def constants():
    per = SIDE * MOST
    r = np.arange(2 * SIDE * per)
    plane, place = r // (2 * per), r % MOST
    slots = np.zeros((2, 2, len(r), 128))
    for h in range(2):
        for d in range(2):
            slots[h, d, r, (2 * plane + h) * MOST + place + 64 * d] = 1
    return jnp.asarray(slots, BF16)


def sixth(i):
    return (i * 683) >> 12


def one_hot(shape, place):
    row = lax.broadcasted_iota(jnp.int32, shape, 0)
    col = lax.broadcasted_iota(jnp.int32, shape, 1)
    return jnp.where(place(row, col), 1.0, 0.0).astype(BF16)


N_SEMS = 128


def kernel(
    acts, grads, saved_in, gain_in, gate_w, up_w, down_w, fr_in, fg_in, br_in, bg_in, slot_in,
    out_ref,
    saved_ref, gain_ref, f_routes, f_gates, b_routes, b_gates, slot_of,
    in_buf, cot_buf, norm_buf, tab, ytok, zsend, xbuf, rbuf, w1, wd, part, d_part, psend, precv,
    psend_c, precv_c, act, dgu, mine, rsopp, rsrecv, rssend, rsin, zpack, zret, ypack, yret,
    pick, pick_t, row_mask, token_mask,
    send_sem, recv_sem, copy_sem,
):
    tokens, width = saved_ref.shape[1], saved_ref.shape[2]
    half_d, chunk = width // 2, width // 4
    rows = rbuf.shape[1]
    block = rows // SIDE
    per = block // SIDE
    hid = wd.shape[0] // 2
    packed_rows = 2 * block
    pipe = lax.axis_index("pipe")
    n_pipe = lax.axis_size("pipe")
    me = lax.axis_index("expert")
    z, y, x = me // (SIDE * SIDE), me // SIDE % SIDE, me % SIDE
    h, yl = y // 2, y % 2
    other = 1 - yl

    def at(zz, yy, xx):
        return (pipe, (zz * SIDE + yy) * SIDE + xx)

    ahead, behind = (lax.rem(pipe + 1, n_pipe), me), (lax.rem(pipe + n_pipe - 1, n_pipe), me)
    zi = [z, z + 1 - 2 * (z % 2), lax.rem(z + 2, SIDE), SIDE - 1 - z]
    ys = [y, y + 1 - 2 * (y % 2), SIDE - 1 - y, lax.rem(y + 2, SIDE)]
    xr, xo, xl = (lax.rem(x + k, SIDE) for k in (1, 2, 3))
    right, left = at(z, y, xr), at(z, y, xl)
    mate = at(z, h * 2 + other, x)
    z_peers = [at(zi[k], y, x) for k in (1, 2, 3)]
    y_peers = [at(z, ys[k], x) for k in (1, 2, 3)]

    barrier = pltpu.get_barrier_semaphore()
    peers = [ahead, behind, right, left] + z_peers + y_peers
    for p in peers:
        pl.semaphore_signal(barrier, inc=1, device_id=p, device_id_type=pl.DeviceIdType.MESH)

    started = []

    def send(src, dst, to):
        i = len(started)
        c = pltpu.make_async_remote_copy(
            src_ref=src, dst_ref=dst, send_sem=send_sem.at[i], recv_sem=recv_sem.at[i],
            device_id=to, device_id_type=pl.DeviceIdType.MESH,
        )
        c.start()
        started.append(c)
        return c

    local = []

    def fetch(src, dst):
        c = pltpu.make_async_copy(src, dst, copy_sem.at[len(local)])
        c.start()
        local.append(c)
        return c

    F, B, C = 0, 1, 2

    inputs = [
        fetch(src, dst)
        for src, dst in (
            (fr_in, f_routes), (fg_in, f_gates), (br_in, b_routes), (bg_in, b_gates),
            (slot_in.at[h], slot_of), (saved_in, saved_ref), (gain_in, gain_ref),
        )
    ]
    for c in inputs:
        c.wait()

    eye = lax.broadcasted_iota(jnp.int32, (tokens, tokens), 0) == lax.broadcasted_iota(
        jnp.int32, (tokens, tokens), 1)
    before = lax.broadcasted_iota(jnp.int32, (tokens, tokens), 0) > lax.broadcasted_iota(
        jnp.int32, (tokens, tokens), 1)
    lane = lax.broadcasted_iota(jnp.int32, (tokens, 128), 1)
    is_f = lane < 64
    lane64 = lane & 63
    lane_expert = (lane64 * 43) >> 8
    lane_place = lane64 - lane_expert * MOST

    def column(ref, k):
        return jnp.sum(jnp.where(eye, ref[0, k:k + 1, :].astype(F32), 0.0), axis=1, keepdims=True)

    le = lane_expert.astype(F32)
    weight, named = 0.0, 0.0
    for k in range(2):
        hit = le == jnp.where(is_f, column(f_routes, k), column(b_routes, k))
        weight = weight + jnp.where(hit, jnp.where(is_f, column(f_gates, k), column(b_gates, k)), 0.0)
        named = named + jnp.where(hit, 1.0, 0.0)
    earlier = dot(jnp.where(before, 1.0, 0.0).astype(BF16), named.astype(BF16))
    tab[y] = jnp.where(earlier == lane_place.astype(F32), weight, 0.0)

    def scale_of(v):
        return lax.rsqrt(jnp.mean(v * v, axis=-1, keepdims=True) + EPS)

    gain = gain_ref[...]

    def d_half(k):
        return pl.ds(pl.multiple_of(k * half_d, half_d), half_d)

    def y_spread(a, ref):
        cs = [
            send(ref.at[:, d_half(ys[k] % 2)], ytok.at[a, y], y_peers[k - 1]) for k in (1, 2, 3)
        ]
        ytok[a, y] = ref[:, d_half(yl)]
        return cs

    def unpacked(i, c):
        return i + (sixth(i) >> 2) * per + c * per

    def z_spread(a, cy):
        for c in cy:
            c.wait_recv()
        got = 0.0
        for c in range(2):
            toks = ytok[a, :, :, c * chunk:(c + 1) * chunk].reshape(SIDE * tokens, chunk)
            got = got + dot(selects[0 if a == F else 1][c], toks)
        zsend[a] = got.astype(BF16).reshape(zsend.shape[1:])
        cs = [send(zsend.at[a, zi[k]], xbuf.at[a, x, z], z_peers[k - 1]) for k in (1, 2, 3)]
        xbuf[a, x, z] = zsend[a, z]
        return [None] + cs

    xs = [[None] * SIDE for _ in range(3)]
    xf = [[], [], []]

    def x_send(a, i, cz):
        if i > 0:
            cz[i].wait_recv()
        ref = xbuf.at[a, x, zi[i]]
        xs[a][i] = (send(ref, ref, right), send(ref, ref, left))

    def x_forward(a, i):
        xs[a][i][i % 2].wait_recv()
        ref = xbuf.at[a, (xl, xr)[i % 2], zi[i]]
        xf[a].append(send(ref, ref, (right, left)[i % 2]))

    def gathered(a):
        for i in range(SIDE):
            xs[a][i][1 - i % 2].wait_recv()
        for c in xf[a]:
            c.wait_recv()
        for s in range(SIDE):
            packed = xbuf[a, s].reshape(packed_rows, chunk)
            for c in range(2):
                rbuf[a, s * block:(s + 1) * block, c * chunk:(c + 1) * chunk] = dot(
                    pick[c], packed).astype(BF16)

    v = saved_ref[0].astype(F32)
    norm_buf[B] = (v * scale_of(v) * gain).astype(BF16)
    pl.semaphore_wait(barrier, len(peers))

    c_acts = send(acts.at[0], in_buf, ahead)
    c_grads = send(grads.at[0], cot_buf, behind)
    c_tab = [send(tab.at[y], tab.at[y], p) for p in y_peers]
    cy = {B: y_spread(B, norm_buf.at[B])}

    def hidden(k):
        return pl.ds(pl.multiple_of(k * hid, hid), hid)

    def weight_rows(ref, lane0, k):
        rows_k = pl.ds(pl.multiple_of(other * half_d + k * chunk, chunk), chunk)
        dst = w1.at[yl, k * chunk:(k + 1) * chunk, lane0:lane0 + hid]
        return send(ref.at[0, rows_k, :], dst, mate)

    c_gu = [weight_rows(gate_w, 0, 0)]
    def down_piece(q):
        n = hid // SIDE
        rows_q = pl.ds(pl.multiple_of(yl * hid + q * n, n), n)
        return send(down_w.at[0, q * n:(q + 1) * n, d_half(other)], wd.at[rows_q, :], mate)

    f_gu = [fetch(gate_w.at[0, d_half(yl), :], w1.at[yl, :, 0:hid]),
            fetch(up_w.at[0, d_half(yl), :], w1.at[yl, :, hid:2 * hid])]
    f_d = fetch(down_w.at[0, :, d_half(yl)], wd.at[hidden(yl), :])

    def matches(shape, dim, c):
        row = lax.broadcasted_iota(jnp.int32, shape, dim)
        token = lax.broadcasted_iota(jnp.int32, shape, 1 - dim)
        return ((sixth(row) >> 2) & 1 == c) & (sixth(row) & 3 == token // tokens)

    for c in range(2):
        row_mask[c] = jnp.where(matches(row_mask.shape[1:], 0, c), 1.0, 0.0).astype(BF16)
        token_mask[c] = jnp.where(matches(token_mask.shape[1:], 1, c), 1.0, 0.0).astype(BF16)
        pick[c] = one_hot(pick.shape[1:], lambda i, j: j == unpacked(i, c))
        pick_t[c] = one_hot(pick_t.shape[1:], lambda i, j: i == unpacked(j, c))

    for c in c_tab:
        c.wait_recv()
    table = tab[...].reshape(SIDE * tokens, 128)
    chosen = jnp.where(table > 0, 1.0, 0.0).astype(BF16)
    w_hi = table.astype(BF16)
    w_lo = (table - w_hi.astype(F32)).astype(BF16)

    selects = [
        [dot_t(slot_of[d], chosen).astype(BF16) * row_mask[c] for c in range(2)]
        for d in range(2)
    ]

    cz = {B: z_spread(B, cy[B])}
    x_send(B, 0, cz[B])
    c_acts.wait_recv()
    v = in_buf[...].astype(F32)
    norm_buf[F] = (v * scale_of(v) * gain).astype(BF16)
    cy[F] = y_spread(F, norm_buf.at[F])
    c_grads.wait_recv()
    cy[C] = y_spread(C, cot_buf)
    c_gu += [weight_rows(gate_w, 0, 1), weight_rows(up_w, hid, 0), weight_rows(up_w, hid, 1)]
    c_d = [down_piece(q) for q in (0, 1)]
    x_send(B, 1, cz[B])
    x_forward(B, 0)
    x_send(B, 2, cz[B])
    cz[F] = z_spread(F, cy[F])
    x_send(F, 0, cz[F])
    x_forward(B, 1)
    x_send(B, 3, cz[B])
    cz[C] = z_spread(C, cy[C])
    x_send(C, 0, cz[C])
    x_forward(B, 2)
    x_send(F, 1, cz[F])
    x_forward(B, 3)
    x_forward(F, 0)
    x_send(F, 2, cz[F])
    x_forward(F, 1)
    x_send(F, 3, cz[F])
    x_forward(C, 0)
    x_forward(F, 2)
    x_send(C, 1, cz[C])
    x_forward(F, 3)
    x_send(C, 2, cz[C])
    x_forward(C, 1)
    x_send(C, 3, cz[C])
    gathered(B)

    order = (xo, xr, xl, x)

    def pair(src, dst):
        return [send(src.at[k], dst.at[k], mate) for k in order]

    def in_blocks(v):
        return v.reshape(SIDE, block, v.shape[1])

    gathered(F)
    for c in f_gu:
        c.wait()
    for c in c_gu:
        c.wait_recv()
    cp = {}
    psend[F] = in_blocks(dot(rbuf[F], w1[other])).astype(BF16)
    cp[F] = pair(psend.at[F], precv.at[F])
    c_d += [down_piece(q) for q in (2, 3)]
    part[F] = in_blocks(dot(rbuf[F], w1[yl]))
    x_forward(C, 2)

    c_act = []
    for n, k in enumerate(order):
        cp[F][n].wait_recv()
        gu = part[F, k] + precv[F, k].astype(F32)
        gate, up = gu[:, :hid], gu[:, hid:]
        act[yl, k] = (gate * jax.nn.sigmoid(gate) * up).astype(BF16)
        c_act.append(send(act.at[yl, k], act.at[yl, k], mate))
        if n == 0:
            x_forward(C, 3)

    psend[B] = in_blocks(dot(rbuf[B], w1[other])).astype(BF16)
    part[B] = in_blocks(dot(rbuf[B], w1[yl]))

    to_right, to_left = (2, 1), (3, 0)

    def reduce_start(d, block_of, ready):
        ready[0].wait_recv()
        rsopp[d] = block_of(xo).astype(BF16).reshape(rsopp.shape[1:])
        opp, got = {}, ({}, {})
        for i, j in zip(to_right, to_left):
            opp[i] = send(rsopp.at[d, zi[i]], rsrecv.at[d, zi[i]], right)
            opp[j] = send(rsopp.at[d, zi[j]], rsrecv.at[d, zi[j]], left)
        for n, (k, to, now) in enumerate(((xr, right, to_left), (xl, left, to_right))):
            ready[n + 1].wait_recv()
            mine[d, n] = block_of(k).reshape(mine.shape[2:])
            for i in now:
                rssend[d, n, zi[i]] = mine[d, n, zi[i]].astype(BF16)
                got[n][i] = send(rssend.at[d, n, zi[i]], rsin.at[d, n, zi[i]], to)
        ready[3].wait_recv()
        mine[d, 2] = block_of(x).reshape(mine.shape[2:])
        return opp, got

    def reduce_finish(d, cr):
        opp, got = cr
        for pair in zip(to_right, to_left):
            for n, (i, to) in enumerate(zip(pair, (right, left))):
                opp[i].wait_recv()
                total = mine[d, n, zi[i]] + rsrecv[d, zi[i]].astype(F32)
                rssend[d, n, zi[i]] = total.astype(BF16)
                got[n][i] = send(rssend.at[d, n, zi[i]], rsin.at[d, n, zi[i]], to)
        return got

    def z_return(d, got):
        cs = []
        for i in (2, 3, 1, 0):
            got[0][i].wait_recv()
            got[1][i].wait_recv()
            total = mine[d, 2, zi[i]] + rsin[d, 0, zi[i]].astype(F32) + rsin[d, 1, zi[i]].astype(F32)
            if i == 0:
                zret[d, z] = total.astype(BF16)
            else:
                zpack[d, zi[i]] = total.astype(BF16)
                cs.append(send(zpack.at[d, zi[i]], zret.at[d, z], at(zi[i], y, x)))
        return cs

    def y_return(d, cr):
        weighs = [
            [dot_t(w, slot_of[d]).astype(BF16) * token_mask[c] for w in (w_hi, w_lo)]
            for c in range(2)
        ]
        for c in cr:
            c.wait_recv()
        slots = zret[d].reshape(packed_rows, chunk)
        for c in range(2):
            got = dot(weighs[c][0], slots) + dot(weighs[c][1], slots)
            ypack[d, :, :, c * chunk:(c + 1) * chunk] = got.astype(BF16).reshape(SIDE, tokens, chunk)
        cs = [send(ypack.at[d, ys[k]], yret.at[d, h, :, d_half(yl)], y_peers[k - 1]) for k in (1, 2, 3)]
        yret[d, h, :, d_half(yl)] = ypack[d, y]
        return cs

    def combine(d, cr):
        for c in cr:
            c.wait_recv()
        return yret[d, 0].astype(F32) + yret[d, 1].astype(F32)

    gathered(C)
    f_d.wait()
    for c in c_d:
        c.wait_recv()
    psend_c[...] = in_blocks(dot_t(rbuf[C], wd[hidden(other), :])).astype(BF16)
    cp[C] = pair(psend_c, precv_c)
    cp[B] = pair(psend.at[B], precv.at[B])
    d_part[...] = in_blocks(dot_t(rbuf[C], wd[hidden(yl), :]))

    def f_block(k):
        a = jnp.concatenate([act[0, k], act[1, k]], axis=1)
        total = 0.0
        for c in range(2):
            total = total + dot(dot(pick_t[c], a).astype(BF16), wd[:, c * chunk:(c + 1) * chunk])
        return total

    cr_f = reduce_start(0, f_block, c_act)
    cr_f = reduce_finish(0, cr_f)

    c_dgu = []
    for n, k in enumerate(order):
        cp[C][n].wait_recv()
        cp[B][n].wait_recv()
        gu = part[B, k] + precv[B, k].astype(F32)
        gate, up = gu[:, :hid], gu[:, hid:]
        sigma = jax.nn.sigmoid(gate)
        d_act = d_part[k] + precv_c[k].astype(F32)
        dgu[yl, k, :, 0:hid] = (d_act * up * sigma * (1.0 + gate * (1.0 - sigma))).astype(BF16)
        dgu[yl, k, :, hid:2 * hid] = (d_act * gate * sigma).astype(BF16)
        c_dgu.append(send(dgu.at[yl, k], dgu.at[yl, k], mate))

    def b_block(k):
        total = 0.0
        for s in range(2):
            for c in range(2):
                a = dot(pick_t[c], dgu[s, k]).astype(BF16)
                total = total + dot_t(a, w1[s, c * chunk:(c + 1) * chunk, :])
        return total

    cr_b = reduce_start(1, b_block, c_dgu)
    cr_f = z_return(0, cr_f)
    cr_b = reduce_finish(1, cr_b)
    cr_f = y_return(0, cr_f)
    cr_b = z_return(1, cr_b)

    out_ref[0] = (in_buf[...].astype(F32) + combine(0, cr_f)).astype(BF16)

    cr_b = y_return(1, cr_b)
    v = saved_ref[0].astype(F32)
    scale = scale_of(v)
    dn = combine(1, cr_b) * gain
    d_in = scale * dn - v * (scale * scale * scale) * jnp.mean(dn * v, axis=-1, keepdims=True)
    out_ref[1] = (cot_buf[...].astype(F32) + d_in).astype(BF16)

    for c in started:
        c.wait_send()


def local(*args):
    held_acts = args[0]
    tokens, width = held_acts.shape[1:]
    hid = args[4].shape[2]
    per = SIDE * MOST
    block = SIDE * per
    rows = SIDE * block
    half_d, chunk = width // 2, width // 4
    args = args[:7] + tuple(jnp.swapaxes(a, 1, 2) for a in args[7:])
    vmem, hbm = pl.BlockSpec(memory_space=pltpu.VMEM), pl.BlockSpec(memory_space=pl.ANY)
    out = jax.ShapeDtypeStruct((2, tokens, width), BF16)
    slots = constants()
    V = pltpu.VMEM
    packed = (SIDE, 2 * per, chunk)
    both = pl.pallas_call(
        kernel,
        out_shape=out,
        in_specs=[hbm] * 12,
        out_specs=vmem,
        scratch_shapes=[
            V(args[2].shape, BF16),
            V(args[3].shape, F32),
            V(args[7].shape, jnp.int32),
            V(args[8].shape, F32),
            V(args[9].shape, jnp.int32),
            V(args[10].shape, F32),
            V(slots.shape[1:], BF16),
            V((tokens, width), BF16),
            V((tokens, width), BF16),
            V((2, tokens, width), BF16),
            V((SIDE, tokens, 128), F32),
            V((3, SIDE, tokens, half_d), BF16),
            V((3,) + packed, BF16),
            V((3, SIDE) + packed, BF16),
            V((3, rows, half_d), BF16),
            V((2, half_d, 2 * hid), BF16),
            V((2 * hid, half_d), BF16),
            V((2, SIDE, block, 2 * hid), F32),
            V((SIDE, block, hid), F32),
            V((2, SIDE, block, 2 * hid), BF16),
            V((2, SIDE, block, 2 * hid), BF16),
            V((SIDE, block, hid), BF16),
            V((SIDE, block, hid), BF16),
            V((2, SIDE, block, hid), BF16),
            V((2, SIDE, block, 2 * hid), BF16),
            V((2, 3) + packed, F32),
            V((2,) + packed, BF16),
            V((2,) + packed, BF16),
            V((2, 2) + packed, BF16),
            V((2, 2) + packed, BF16),
            V((2,) + packed, BF16),
            V((2,) + packed, BF16),
            V((2, SIDE, tokens, half_d), BF16),
            V((2, 2, tokens, width), BF16),
            V((2, block, 2 * block), BF16),
            V((2, 2 * block, block), BF16),
            V((2, 2 * block, SIDE * tokens), BF16),
            V((2, SIDE * tokens, 2 * block), BF16),
            pltpu.SemaphoreType.DMA((N_SEMS,)),
            pltpu.SemaphoreType.DMA((N_SEMS,)),
            pltpu.SemaphoreType.DMA((10,)),
        ],
        compiler_params=pltpu.CompilerParams(
            collective_id=0, has_side_effects=True, vmem_limit_bytes=58 * 1024 * 1024
        ),
    )(*args, slots)
    return both[0:1], both[1:2]


def solution(mesh):
    return jax.shard_map(
        local,
        mesh=mesh,
        in_specs=(
            P("pipe", "expert", None),
            P("pipe", "expert", None),
            P("pipe", "expert", None),
            P("pipe", None),
            P("pipe", None, "expert"),
            P("pipe", None, "expert"),
            P("pipe", "expert", None),
            P("pipe", "expert", None),
            P("pipe", "expert", None),
            P("pipe", "expert", None),
            P("pipe", "expert", None),
        ),
        out_specs=(P("pipe", "expert", None), P("pipe", "expert", None)),
        check_vma=False,
    )
```
